32 devices in a mesh: parts: 2 (over x), chain: 16 (over z, y, core).
Axes of the slice: x: 2, y: 2, z: 4, core: 2. Of those that a mesh axis runs over, the one named last changes fastest.
Arguments:
- subspace: float32 [64, 8192], P('parts', 'chain'), parts along dimension 0, may hold values from -4 to 4
- s_inv: float32 [8, 32, 2, 256, 256], P('parts', 'chain'), parts along dimension 0, may hold values from -1 to 1
- couple: float32 [32, 512, 256], P('chain', 'parts'), parts along dimension 1, may hold values from -1 to 1
- diag_blocks: float32 [32, 512, 256], P('chain', 'parts'), parts along dimension 1, may hold values from -4 to 4
- weights: float32 [8, 2], P('parts'), parts along dimension 0, may hold values from -1 to 1
Outputs:
- filtered: float32 [64, 8192], P('parts', 'chain'), parts along dimension 0
- applied: float32 [64, 8192], P('parts', 'chain'), parts along dimension 0
- grams: float32 [2, 64, 32], P(None, 'parts'), parts along dimension 1
The draws below stay inside these ranges and needn't reach their ends.
There are 2 independent parts, one for each index of `parts`. The reference program is written for one: setup_inputs(seed, part) draws one part's arguments, and reference() takes and returns one part's arrays. A program takes and returns all parts, laid end to end along the dimension named above; each array names one. Nothing has to cross between parts.
All inputs are finite; a program needn't handle non-finite values.
Results may differ from the reference program's by a relative error of at most 0.00027.
Values sent between devices are 32-bit elements; how exact they have to be, the bound alone decides.
A program may use at most 192 MiB of HBM per device.

```python
import math
import jax
import jax.numpy as jnp
from jax import lax

KB = 256
NV = 32
QUAD = 4
NB = 32
ORDER = 8192


def draw_s_inv(key, part):
    subkeys = jax.random.split(key, 3)
    full_shape = (QUAD, NB, 2, KB, KB)
    row_ids = lax.broadcasted_iota(jnp.int32, full_shape, 3)
    col_ids = lax.broadcasted_iota(jnp.int32, full_shape, 4)
    identity = (row_ids == col_ids).astype(jnp.float32)
    component = lax.broadcasted_iota(jnp.int32, full_shape, 2)
    spread = jnp.clip(jax.random.normal(subkeys[0], full_shape, jnp.float32), -4.0, 4.0)
    target = math.exp(-2.0 / NB)
    center = math.sqrt(target - 0.21)
    real_diag = center * jax.random.uniform(subkeys[1], (QUAD, NB, 1, KB, 1), jnp.float32, 0.9, 1.1)
    imag_diag = jax.random.uniform(subkeys[2], (QUAD, NB, 1, KB, 1), jnp.float32, -0.3, 0.3)
    diagonal = jnp.where(component == 0, real_diag, imag_diag)
    values = 0.3 * KB ** (-0.5) * spread + identity * diagonal
    return jnp.clip(values, -1.0, 1.0)


def draw_couple(key, part):
    subkeys = jax.random.split(key, 1)
    full_shape = (NB, KB, KB)
    spread = jnp.clip(jax.random.normal(subkeys[0], full_shape, jnp.float32), -4.0, 4.0)
    return jnp.clip(KB ** (-0.5) * spread, -1.0, 1.0)


def draw_diag_blocks(key, part):
    subkeys = jax.random.split(key, 2)
    full_shape = (NB, KB, KB)
    row_ids = lax.broadcasted_iota(jnp.int32, full_shape, 1)
    col_ids = lax.broadcasted_iota(jnp.int32, full_shape, 2)
    identity = (row_ids == col_ids).astype(jnp.float32)
    spread = jnp.clip(jax.random.normal(subkeys[0], full_shape, jnp.float32), -4.0, 4.0)
    diagonal = jnp.exp(jax.random.uniform(subkeys[1], (NB, KB, 1), jnp.float32, -0.6931472, 1.3862944))
    values = 0.5 * KB ** (-0.5) * spread + identity * diagonal
    return jnp.clip(values, -4.0, 4.0)


def draw_subspace(key, part):
    subkeys = jax.random.split(key, 3)
    full_shape = (NV, ORDER)
    position = jnp.arange(ORDER, dtype=jnp.float32) / ORDER
    row_trend = jnp.exp(1.0986123 * (position - 0.5))[None, :]
    row_scale = jnp.exp(jax.random.uniform(subkeys[1], (1, ORDER), jnp.float32, -1.1512925, 1.1512925))
    col_scale = jnp.exp(jax.random.uniform(subkeys[2], (NV, 1), jnp.float32, -1.1512925, 1.1512925))
    base_draw = jnp.clip(jax.random.normal(subkeys[0], full_shape, jnp.float32), -4.0, 4.0)
    return jnp.clip(2.0 / NB * base_draw * row_trend * row_scale * col_scale, -4.0, 4.0)


def setup_inputs(seed: int = 0, part: int = 0) -> dict:
    streams_of = jax.random.split(jax.random.key(seed), 6)
    own_keys = jax.random.split(jax.random.fold_in(streams_of[5], part), 6)
    return {
        "subspace": draw_subspace(jax.random.fold_in(jax.random.fold_in(streams_of[5], part), 71), part),
        "s_inv": draw_s_inv(jax.random.fold_in(jax.random.fold_in(streams_of[5], part), 71), part),
        "couple": draw_couple(jax.random.fold_in(jax.random.fold_in(streams_of[5], part), 71), part),
        "diag_blocks": draw_diag_blocks(jax.random.fold_in(jax.random.fold_in(streams_of[5], part), 71), part),
        "weights": jnp.clip(jax.random.uniform(own_keys[4], (QUAD, 2), jnp.float32, -1.0, 1.0), -1.0, 1.0),
    }


highest = lax.Precision.HIGHEST


def inverse_apply(pivot_inv, vecs):
    real_part = jnp.einsum("qnk,qjk->qnj", vecs[:, 0], pivot_inv[:, 0], precision=highest) - jnp.einsum("qnk,qjk->qnj", vecs[:, 1], pivot_inv[:, 1], precision=highest)
    imag_part = jnp.einsum("qnk,qjk->qnj", vecs[:, 0], pivot_inv[:, 1], precision=highest) + jnp.einsum("qnk,qjk->qnj", vecs[:, 1], pivot_inv[:, 0], precision=highest)
    return jnp.stack([real_part, imag_part], axis=1)


def couple_down(coupling_blk, vecs):
    return jnp.einsum("qcnk,kj->qcnj", vecs, coupling_blk, precision=highest)


def couple_up(coupling_blk, vecs):
    return jnp.einsum("qcnk,jk->qcnj", vecs, coupling_blk, precision=highest)


def reference(subspace, s_inv, couple, diag_blocks, weights):
    points = s_inv.shape[0]
    blocks_all = couple.shape[0]
    block_width = couple.shape[1]
    vectors = subspace.shape[0]
    source = subspace.reshape(vectors, blocks_all, block_width).transpose(1, 0, 2)
    pivots = jnp.moveaxis(s_inv, 1, 0)
    zero_state = jnp.zeros((points, 2, vectors, block_width), jnp.float32)

    def forward(carried, scanned):
        pivot_inv, coupling_blk, rhs_block = scanned
        combined = carried.at[:, 0].add(rhs_block[None])
        solved = inverse_apply(pivot_inv, combined)
        return couple_down(coupling_blk, solved), solved

    _, solved_all = lax.scan(forward, zero_state, (pivots, couple, source))

    def backward(carried, scanned):
        pivot_inv, coupling_blk, known = scanned
        updated = known + inverse_apply(pivot_inv, couple_up(coupling_blk, carried))
        return updated, updated

    _, result = lax.scan(backward, zero_state, (pivots, couple, solved_all), reverse=True)
    signed = weights * jnp.array([1.0, -1.0], jnp.float32)
    filtered_blocks = jnp.einsum("rqcnk,qc->rnk", result, signed, precision=highest)
    diag_term = jnp.einsum("rnk,rjk->rnj", filtered_blocks, diag_blocks, precision=highest)
    upper_rows = jnp.concatenate([filtered_blocks[1:], jnp.zeros_like(filtered_blocks[:1])], axis=0)
    term_up = jnp.einsum("rnk,rjk->rnj", upper_rows, couple, precision=highest)
    down_all = jnp.einsum("rnk,rkj->rnj", filtered_blocks, couple, precision=highest)
    lower_rows = jnp.concatenate([jnp.zeros_like(down_all[:1]), down_all[:-1]], axis=0)
    applied_blocks = diag_term + term_up + lower_rows
    gram_plain = jnp.einsum("rnk,rmk->nm", filtered_blocks, filtered_blocks, precision=highest)
    gram_matrix = jnp.einsum("rnk,rmk->nm", filtered_blocks, applied_blocks, precision=highest)
    order_total = blocks_all * block_width
    grams = jnp.stack([gram_plain, gram_matrix]) / order_total
    filtered = filtered_blocks.transpose(1, 0, 2).reshape(vectors, order_total)
    applied = applied_blocks.transpose(1, 0, 2).reshape(vectors, order_total)
    return filtered, applied, grams
```

```python
import functools

import jax
import jax.numpy as jnp
from jax import lax
from jax.experimental import pallas as pl
from jax.experimental.pallas import tpu as pltpu
from jax.sharding import PartitionSpec as P

MESH = pl.DeviceIdType.MESH
f32, bf16 = jnp.float32, jnp.bfloat16
NT = (((1,), (1,)), ((), ()))
NN = (((1,), (0,)), ((), ()))


def split(a):
    high = a.astype(bf16)
    return high, (a - high.astype(f32)).astype(bf16)


def dot(a, b, dims):
    return lax.dot_general(a, b, dims, preferred_element_type=f32)


def product(a, b, dims):
    return dot(a[0], b[0], dims) + (dot(a[0], b[1], dims) + dot(a[1], b[0], dims))


def apply_map(rows, high, low):
    half, width = rows.shape[0] // 2, rows.shape[1]
    rows_high, rows_low = split(rows)
    both = dot(jnp.concatenate([rows_high, rows_low], axis=0), high, NT)
    mixed = both[: 2 * half] + (both[2 * half :] + dot(rows_high, low, NT))
    results = []
    for at in range(0, mixed.shape[1], 2 * width):
        by_re, by_im = mixed[:, at : at + width], mixed[:, at + width : at + 2 * width]
        results.append(
            jnp.concatenate([by_re[:half] - by_im[half:], by_re[half:] + by_im[:half]], axis=0)
        )
    return results


def compose(a, b):
    width = b[0].shape[1]
    by_re = product(a, (b[0][:width], b[1][:width]), NN)
    by_im = product(a, (b[0][width:], b[1][width:]), NN)
    return jnp.concatenate([by_re[:width] - by_im[width:], by_im[:width] + by_re[width:]], axis=0)


def kernel(
    n, f_hbm, s_hbm, e_hbm, d_hbm, w_ref, filt_ref, app_ref, gram_ref,
    F, S, E, D, Eh, El, Th, Tl, Wh, Wl, Nh, Nl, Ch, Cl, Rh, Rl,
    tip, cin, cout, y, u, xin, xout, pf, pfin, ff, fnext, fsend, down, downin,
    gown, gin, gsib, gfin, local_sem, swap_send, swap_recv, fwd_send, fwd_recv,
    bwd_send, bwd_recv, one_send, one_recv, all_send, all_recv,
):
    me = lax.axis_index("chain")
    chip, core = lax.div(me, 2), lax.rem(me, 2)
    sib = chip * 2 + 1 - core
    after = jnp.minimum(chip + 1, n - 1) * 2 + core
    before = jnp.maximum(chip - 1, 0) * 2 + core
    right = jnp.minimum(me + 1, 2 * n - 1)
    left = jnp.maximum(me - 1, 0)
    first, last = chip == 0, chip == n - 1
    points, blocks = S.shape[0], S.shape[1]
    mine = e_hbm.shape[0]
    width = e_hbm.shape[1]
    vectors = f_hbm.shape[0]

    def greet(device):
        pl.semaphore_signal(barrier, inc=1, device_id={"chain": device}, device_id_type=MESH)

    def remote(src, dst, send, recv, device):
        return pltpu.make_async_remote_copy(
            src_ref=src, dst_ref=dst, send_sem=send, recv_sem=recv,
            device_id={"chain": device}, device_id_type=MESH,
        )

    here = pl.ds(core * mine, mine)
    own_points = pl.ds(core * points, points)
    sib_points = pl.ds((1 - core) * points, points)
    local = [
        pltpu.make_async_copy(f_hbm, F.at[core], local_sem.at[0]),
        pltpu.make_async_copy(e_hbm, E.at[here], local_sem.at[1]),
        pltpu.make_async_copy(s_hbm.at[own_points], S.at[:, here], local_sem.at[2]),
        pltpu.make_async_copy(d_hbm, D, local_sem.at[3]),
    ]
    for copy in local:
        copy.start()

    barrier = pltpu.get_barrier_semaphore()
    greet(sib)

    @pl.when(jnp.logical_not(first))
    def _():
        greet(before)
        greet(core)

    @pl.when(jnp.logical_not(last))
    def _():
        greet(after)

    @pl.when(jnp.logical_and(core == 0, jnp.logical_not(first)))
    def _():
        greet(left)

    @pl.when(jnp.logical_and(core == 1, jnp.logical_not(last)))
    def _():
        greet(right)

    has_next = jnp.where(last, 0, 1)
    has_prev = jnp.where(first, 0, 1)
    pl.semaphore_wait(
        barrier,
        1 + has_next + has_prev + jnp.where(core == 1, has_next, has_prev)
        + jnp.where(first, n - 1, 0),
    )
    swap = [
        remote(f_hbm, F.at[core], swap_send.at[0], swap_recv.at[0], sib),
        remote(e_hbm, E.at[here], swap_send.at[1], swap_recv.at[1], sib),
        remote(s_hbm.at[sib_points], S.at[:, here], swap_send.at[2], swap_recv.at[2], sib),
    ]
    for copy in swap:
        copy.start()
    for copy in local:
        copy.wait()
    for copy in swap:
        copy.wait()

    @pl.loop(0, blocks)
    def _(b):
        Eh[b], El[b] = split(E[b])
        Th[b], Tl[b] = split(E[b].T)

    @pl.loop(0, points)
    def _(q):
        @pl.loop(0, blocks)
        def _(b):
            high, low = split(S[q, b])
            Wh[q, b, : 2 * width], Wl[q, b, : 2 * width] = high, low
            turned = (Th[b], Tl[b])
            for part in range(2):
                rows = slice(part * width, (part + 1) * width)
                out = split(product(turned, (high[rows], low[rows]), NN))
                to = slice((2 + part) * width, (3 + part) * width)
                Wh[q, b, to], Wl[q, b, to] = out

    def source(b):
        rows = F[b // mine, :, (b % mine) * width : (b % mine + 1) * width]
        return jnp.concatenate([rows, jnp.zeros_like(rows)], axis=0)

    low_rows = slice(2 * width, 4 * width)
    carried = [None] * points
    for b in range(blocks):
        for q in range(points):
            z = source(b) if b == 0 else source(b) + carried[q]
            (carried[q],) = apply_map(z, Wh[q, b, low_rows], Wl[q, b, low_rows])
    for q in range(points):
        tip[q] = carried[q]

    @pl.when(jnp.logical_and(jnp.logical_not(first), jnp.logical_not(last)))
    def _():
        @pl.loop(0, points)
        def _(q):
            Ch[q], Cl[q] = Wh[q, 0, low_rows], Wl[q, 0, low_rows]

            @pl.loop(1, blocks)
            def _(b):
                Ch[q], Cl[q] = split(
                    compose((Wh[q, b, low_rows], Wl[q, b, low_rows]), (Ch[q], Cl[q]))
                )

    forward = [
        remote(cout.at[q], cin.at[q], fwd_send.at[q], fwd_recv.at[q], after) for q in range(points)
    ]
    backward = [
        remote(xout.at[q], xin.at[q], bwd_send.at[q], bwd_recv.at[q], before)
        for q in range(points)
    ]

    def sweep_forward():
        @pl.when(first)
        def _():
            for q in range(points):
                cout[q] = tip[q]
                forward[q].start()
            cin[...] = jnp.zeros_like(cin)

        @pl.when(jnp.logical_not(first))
        def _():
            for q in range(points):
                forward[q].wait_recv()

                @pl.when(jnp.logical_not(last))
                def _():
                    cout[q] = tip[q] + apply_map(cin[q], Ch[q], Cl[q])[0]
                    forward[q].start()

        entering = [cin[q] for q in range(points)]
        for b in range(blocks):
            for q in range(points):
                z = source(b) + entering[q]
                y[q, b], entering[q] = apply_map(z, Wh[q, b], Wl[q, b])

    def backward_maps():
        @pl.loop(0, points)
        def _(q):
            @pl.loop(0, blocks)
            def _(b):
                pivot = (Wh[q, b, : 2 * width], Wl[q, b, : 2 * width])
                Nh[q, b], Nl[q, b] = split(product(pivot, (Eh[b], El[b]), NN))

            @pl.when(jnp.logical_not(last))
            def _():
                Rh[q, blocks - 1], Rl[q, blocks - 1] = Nh[q, blocks - 1], Nl[q, blocks - 1]

                @pl.loop(1, blocks)
                def _(step):
                    b = blocks - 1 - step
                    Rh[q, b], Rl[q, b] = split(
                        compose((Nh[q, b], Nl[q, b]), (Rh[q, b + 1], Rl[q, b + 1]))
                    )

    maps_first = chip * 2 >= n

    @pl.loop(0, 3)
    def _(step):
        @pl.when(step == 1)
        def _():
            sweep_forward()

        @pl.when(step == jnp.where(maps_first, 0, 2))
        def _():
            backward_maps()

    carried = [None] * points
    for b in reversed(range(blocks)):
        for q in range(points):
            if b == blocks - 1:
                carried[q] = y[q, b]
            else:
                carried[q] = y[q, b] + apply_map(carried[q], Nh[q, b], Nl[q, b])[0]
            u[q, b] = carried[q]

    weight_re = [w_ref[core * points + q, 0] for q in range(points)]
    weight_im = [w_ref[core * points + q, 1] for q in range(points)]

    def filtered_part(q, x):
        return weight_re[q] * x[:vectors] - weight_im[q] * x[vectors:]

    @pl.when(last)
    def _():
        for q in range(points):
            xout[q] = u[q, 0]
            backward[q].start()
        for b in range(blocks):
            total = filtered_part(0, u[0, b])
            for q in range(1, points):
                total = total + filtered_part(q, u[q, b])
            pf[b] = total

    @pl.when(jnp.logical_not(last))
    def _():
        for q in range(points):
            backward[q].wait_recv()
            xout[q] = u[q, 0] + apply_map(xin[q], Rh[q, 0], Rl[q, 0])[0]

            @pl.when(jnp.logical_not(first))
            def _():
                backward[q].start()

        for b in range(blocks):
            total = None
            for q in range(points):
                if b == 0:
                    x = xout[q]
                else:
                    x = u[q, b] + apply_map(xin[q], Rh[q, b], Rl[q, b])[0]
                part = filtered_part(q, x)
                total = part if total is None else total + part
            pf[b] = total

    share = remote(pf, pfin, one_send.at[0], one_recv.at[0], sib)
    share.start()
    share.wait_recv()
    ff[...] = pf[...] + pfin[...]

    to_left = remote(fsend, fnext, one_send.at[1], one_recv.at[1], left)
    to_right = remote(down, downin, one_send.at[2], one_recv.at[2], right)
    gives_left = jnp.logical_and(core == 0, jnp.logical_not(first))
    gives_right = jnp.logical_and(core == 1, jnp.logical_not(last))

    @pl.when(gives_left)
    def _():
        fsend[...] = ff[0]
        to_left.start()

    @pl.when(gives_right)
    def _():
        down[...] = product(split(ff[blocks - 1]), (Eh[blocks - 1], El[blocks - 1]), NN)
        to_right.start()
        to_left.wait_recv()

    @pl.when(jnp.logical_not(gives_right))
    def _():
        fnext[...] = jnp.zeros_like(fnext)

    gram_plain = jnp.zeros((vectors, vectors), f32)
    gram_matrix = jnp.zeros((vectors, vectors), f32)
    for j in range(mine):
        at = core * mine + j
        block = ff[at]
        filt_ref[:, j * width : (j + 1) * width] = block
        if j < mine - 1:
            upper = ff[at + 1]
        else:
            upper = jnp.where(core == 0, ff[mine], fnext[...])
        halves = split(block)
        up = product(split(upper), (Eh[at], El[at]), NT)
        up_halves = split(up)
        partial = product(halves, split(D[j]), NT) + up
        gram_plain += product(halves, halves, NT)
        gram_matrix += product(halves, split(partial), NT) + product(up_halves, halves, NT)
        app_ref[:, j * width : (j + 1) * width] = partial

    pair = remote(gown, gsib, one_send.at[4], one_recv.at[4], sib)
    gown[0] = gram_plain
    gown[1] = gram_matrix
    pass_on = remote(gown, gin, one_send.at[3], one_recv.at[3], before)

    @pl.when(jnp.logical_not(last))
    def _():
        pass_on.wait_recv()
        gown[...] = gown[...] + gin[...]

    @pl.when(jnp.logical_not(first))
    def _():
        pass_on.start()

    @pl.when(first)
    def _():
        pair.start()
        pair.wait_recv()
        scale = 1.0 / (blocks * width * n)
        gfin[...] = (gown[...] + gsib[...]) * scale

        @pl.loop(1, n)
        def _(other):
            remote(gfin, gfin, all_send.at[other], all_recv, other * 2 + core).start()

    for j in range(mine):
        at = core * mine + j
        if j == 0:
            @pl.when(core == 1)
            def _():
                below = product(split(ff[mine - 1]), (Eh[mine - 1], El[mine - 1]), NN)
                app_ref[:, :width] += below

            @pl.when(gives_left)
            def _():
                to_right.wait_recv()
                app_ref[:, :width] += downin[...]
        else:
            below = product(split(ff[at - 1]), (Eh[at - 1], El[at - 1]), NN)
            app_ref[:, j * width : (j + 1) * width] += below

    @pl.when(jnp.logical_not(first))
    def _():
        remote(gfin, gfin, all_send.at[0], all_recv, core).wait_recv()

    gram_ref[...] = gfin[...]

    share.wait_send()

    @pl.when(gives_left)
    def _():
        to_left.wait_send()

    @pl.when(gives_right)
    def _():
        to_right.wait_send()

    @pl.when(jnp.logical_not(last))
    def _():
        for q in range(points):
            forward[q].wait_send()

    @pl.when(jnp.logical_not(first))
    def _():
        for q in range(points):
            backward[q].wait_send()
        pass_on.wait_send()

    @pl.when(first)
    def _():
        pair.wait_send()

        @pl.loop(1, n)
        def _(other):
            remote(gfin, gfin, all_send.at[other], all_recv, other * 2 + core).wait_send()


def shards(n, subspace, s_inv, couple, diag_blocks, weights):
    points, mine = s_inv.shape[0] // 2, s_inv.shape[1]
    width, vectors = couple.shape[1], subspace.shape[0]
    blocks = 2 * mine
    pivots = s_inv.reshape(2 * points, mine, 2 * width, width)
    square = (blocks, width, width)
    maps = (points, blocks, 2 * width, width)
    state = (points, 2 * vectors, width)
    states = (points, blocks, 2 * vectors, width)
    piece = (vectors, width)
    grams = (2, vectors, vectors)
    scratch = (
        [pltpu.VMEM((2, vectors, mine * width), f32), pltpu.VMEM(maps, f32)]
        + [pltpu.VMEM(square, f32), pltpu.VMEM((mine, width, width), f32)]
        + [pltpu.VMEM(square, bf16)] * 4
        + [pltpu.VMEM((points, blocks, 4 * width, width), bf16)] * 2
        + [pltpu.VMEM(maps, bf16)] * 2
        + [pltpu.VMEM((points, 2 * width, width), bf16)] * 2
        + [pltpu.VMEM(maps, bf16)] * 2
        + [pltpu.VMEM(state, f32)] * 3
        + [pltpu.VMEM(states, f32)] * 2
        + [pltpu.VMEM(state, f32)] * 2
        + [pltpu.VMEM((blocks,) + piece, f32)] * 3
        + [pltpu.VMEM(piece, f32)] * 4
        + [pltpu.VMEM(grams, f32)] * 4
        + [pltpu.SemaphoreType.DMA((4,))]
        + [pltpu.SemaphoreType.DMA((3,))] * 2
        + [pltpu.SemaphoreType.DMA((points,))] * 4
        + [pltpu.SemaphoreType.DMA((5,))] * 2
        + [pltpu.SemaphoreType.DMA((n,)), pltpu.SemaphoreType.DMA]
    )
    whole = pl.BlockSpec(memory_space=pltpu.VMEM)
    anywhere = pl.BlockSpec(memory_space=pl.ANY)
    return pl.pallas_call(
        functools.partial(kernel, n),
        out_shape=(
            jax.ShapeDtypeStruct(subspace.shape, f32),
            jax.ShapeDtypeStruct(subspace.shape, f32),
            jax.ShapeDtypeStruct(grams, f32),
        ),
        in_specs=[anywhere] * 4 + [pl.BlockSpec(memory_space=pltpu.SMEM)],
        out_specs=(whole, whole, whole),
        scratch_shapes=scratch,
        compiler_params=pltpu.CompilerParams(
            collective_id=0, has_side_effects=True, vmem_limit_bytes=48 * 2**20
        ),
        name="filter_pass",
    )(subspace, pivots, couple, diag_blocks, weights)


def solution(mesh):
    placed = (
        P("parts", "chain"),
        P("parts", "chain", None, None, None),
        P("chain", "parts", None),
        P("chain", "parts", None),
        P("parts", None),
    )
    return jax.shard_map(
        functools.partial(shards, mesh.shape["chain"] // 2),
        mesh=mesh,
        in_specs=placed,
        out_specs=(P("parts", "chain"), P("parts", "chain"), P(None, "parts", None)),
        check_vma=False,
    )
```

```python
import functools

import jax
import jax.numpy as jnp
from jax import lax
from jax.experimental import pallas as pl
from jax.experimental.pallas import tpu as pltpu
from jax.sharding import PartitionSpec as P

MESH = pl.DeviceIdType.MESH
f32, bf16 = jnp.float32, jnp.bfloat16
NT = (((1,), (1,)), ((), ()))
NN = (((1,), (0,)), ((), ()))


def split(a):
    high = a.astype(bf16)
    return high, (a - high.astype(f32)).astype(bf16)


PIECES = 2


def dot(a, b, dims):
    return lax.dot_general(a, b, dims, preferred_element_type=f32)


def product(a, b, dims):
    return dot(a[0], b[0], dims) + (dot(a[0], b[1], dims) + dot(a[1], b[0], dims))


def apply_map(rows, high, low):
    half, width = rows.shape[0] // 2, rows.shape[1]
    rows_high, rows_low = split(rows)
    both = dot(jnp.concatenate([rows_high, rows_low], axis=0), high, NT)
    mixed = both[: 2 * half] + (both[2 * half :] + dot(rows_high, low, NT))
    results = []
    for at in range(0, mixed.shape[1], 2 * width):
        by_re, by_im = mixed[:, at : at + width], mixed[:, at + width : at + 2 * width]
        results.append(
            jnp.concatenate([by_re[:half] - by_im[half:], by_re[half:] + by_im[:half]], axis=0)
        )
    return results


def joined(parts):
    half = parts[0].shape[0] // 2
    return jnp.concatenate([part[:half] for part in parts] + [part[half:] for part in parts], axis=0)


def piece_of(rows, p):
    half = rows.shape[0] // 2
    size = half // PIECES
    return jnp.concatenate(
        [rows[p * size : (p + 1) * size], rows[half + p * size : half + (p + 1) * size]], axis=0
    )


def compose(a, b):
    width = b[0].shape[1]
    by_re = product(a, (b[0][:width], b[1][:width]), NN)
    by_im = product(a, (b[0][width:], b[1][width:]), NN)
    return jnp.concatenate([by_re[:width] - by_im[width:], by_im[:width] + by_re[width:]], axis=0)


def kernel(
    n, f_hbm, s_hbm, e_hbm, d_hbm, w_hbm, filt_ref, app_ref, gram_ref,
    F, S, E, D, w_ref, Eh, El, Th, Tl, Wh, Wl, Nh, Nl, Ch, Cl, Rh, Rl,
    tip, cin, cout, y, u, xin, xout, pf, pfin, ff, fnext, fsend, down, downin,
    gown, gin, gsib, gfin, local_sem, swap_send, swap_recv, fwd_send, fwd_recv,
    bwd_send, bwd_recv, one_send, one_recv, all_send, all_recv,
):
    me = lax.axis_index("chain")
    chip, core = lax.div(me, 2), lax.rem(me, 2)
    sib = chip * 2 + 1 - core
    after = jnp.minimum(chip + 1, n - 1) * 2 + core
    before = jnp.maximum(chip - 1, 0) * 2 + core
    right = jnp.minimum(me + 1, 2 * n - 1)
    left = jnp.maximum(me - 1, 0)
    first, last = chip == 0, chip == n - 1
    points, blocks = S.shape[0], S.shape[1]
    mine = e_hbm.shape[0]
    width = e_hbm.shape[1]
    vectors = f_hbm.shape[0]

    def greet(device):
        pl.semaphore_signal(barrier, inc=1, device_id={"chain": device}, device_id_type=MESH)

    def remote(src, dst, send, recv, device):
        return pltpu.make_async_remote_copy(
            src_ref=src, dst_ref=dst, send_sem=send, recv_sem=recv,
            device_id={"chain": device}, device_id_type=MESH,
        )

    here = pl.ds(core * mine, mine)
    own_points = pl.ds(core * points, points)
    sib_points = pl.ds((1 - core) * points, points)
    local = [
        pltpu.make_async_copy(f_hbm, F.at[core], local_sem.at[0]),
        pltpu.make_async_copy(e_hbm, E.at[here], local_sem.at[1]),
        pltpu.make_async_copy(s_hbm.at[own_points], S.at[:, here], local_sem.at[2]),
        pltpu.make_async_copy(d_hbm, D, local_sem.at[3]),
        pltpu.make_async_copy(w_hbm, w_ref, local_sem.at[4]),
    ]
    for copy in local:
        copy.start()

    barrier = pltpu.get_barrier_semaphore()
    greet(sib)

    @pl.when(jnp.logical_not(first))
    def _():
        greet(before)
        greet(core)

    @pl.when(jnp.logical_not(last))
    def _():
        greet(after)

    @pl.when(jnp.logical_and(core == 0, jnp.logical_not(first)))
    def _():
        greet(left)

    @pl.when(jnp.logical_and(core == 1, jnp.logical_not(last)))
    def _():
        greet(right)

    has_next = jnp.where(last, 0, 1)
    has_prev = jnp.where(first, 0, 1)
    pl.semaphore_wait(
        barrier,
        1 + has_next + has_prev + jnp.where(core == 1, has_next, has_prev)
        + jnp.where(first, n - 1, 0),
    )
    swap = [
        remote(f_hbm, F.at[core], swap_send.at[0], swap_recv.at[0], sib),
        remote(e_hbm, E.at[here], swap_send.at[1], swap_recv.at[1], sib),
        remote(s_hbm.at[sib_points], S.at[:, here], swap_send.at[2], swap_recv.at[2], sib),
    ]
    for copy in swap:
        copy.start()
    for copy in local:
        copy.wait()

    @pl.loop(0, 2)
    def _(turn):
        @pl.when(turn == 1)
        def _():
            for copy in swap:
                copy.wait()

        start = lax.rem(core + turn, 2) * mine

        @pl.loop(0, mine)
        def _(j):
            b = start + j
            Eh[b], El[b] = split(E[b])
            turned = split(E[b].T)
            Th[b], Tl[b] = turned

            @pl.loop(0, points)
            def _(q):
                high, low = split(S[q, b])
                Wh[q, b, : 2 * width], Wl[q, b, : 2 * width] = high, low
                for part in range(2):
                    rows = slice(part * width, (part + 1) * width)
                    out = split(product(turned, (high[rows], low[rows]), NN))
                    to = slice((2 + part) * width, (3 + part) * width)
                    Wh[q, b, to], Wl[q, b, to] = out

    def source(b):
        rows = F[b // mine, :, (b % mine) * width : (b % mine + 1) * width]
        return jnp.concatenate([rows, jnp.zeros_like(rows)], axis=0)

    low_rows = slice(2 * width, 4 * width)
    carried = [None] * points
    for b in range(blocks):
        for q in range(points):
            z = source(b) if b == 0 else source(b) + carried[q]
            (carried[q],) = apply_map(z, Wh[q, b, low_rows], Wl[q, b, low_rows])
    for q in range(points):
        for p in range(PIECES):
            tip[q, p] = piece_of(carried[q], p)

    @pl.when(jnp.logical_and(jnp.logical_not(first), jnp.logical_not(last)))
    def _():
        @pl.loop(0, points)
        def _(q):
            Ch[q], Cl[q] = Wh[q, 0, low_rows], Wl[q, 0, low_rows]

            @pl.loop(1, blocks)
            def _(b):
                Ch[q], Cl[q] = split(
                    compose((Wh[q, b, low_rows], Wl[q, b, low_rows]), (Ch[q], Cl[q]))
                )

    parts = [(q, p) for q in range(points) for p in range(PIECES)]
    forward = [
        remote(cout.at[at], cin.at[at], fwd_send.at[at], fwd_recv.at[at], after) for at in parts
    ]
    backward = [
        remote(xout.at[at], xin.at[at], bwd_send.at[at], bwd_recv.at[at], before) for at in parts
    ]

    def sweep_forward():
        @pl.when(first)
        def _():
            for at, copy in zip(parts, forward):
                cout[at] = tip[at]
                copy.start()
            cin[...] = jnp.zeros_like(cin)

        @pl.when(jnp.logical_not(first))
        def _():
            for at, copy in zip(parts, forward):
                copy.wait_recv()

                @pl.when(jnp.logical_not(last))
                def _():
                    cout[at] = tip[at] + apply_map(cin[at], Ch[at[0]], Cl[at[0]])[0]
                    copy.start()

        entering = [joined([cin[q, p] for p in range(PIECES)]) for q in range(points)]
        for b in range(blocks):
            for q in range(points):
                z = source(b) + entering[q]
                y[q, b], entering[q] = apply_map(z, Wh[q, b], Wl[q, b])

    def backward_maps():
        @pl.loop(0, points)
        def _(q):
            @pl.loop(0, blocks)
            def _(b):
                pivot = (Wh[q, b, : 2 * width], Wl[q, b, : 2 * width])
                Nh[q, b], Nl[q, b] = split(product(pivot, (Eh[b], El[b]), NN))

            @pl.when(jnp.logical_not(last))
            def _():
                Rh[q, blocks - 1], Rl[q, blocks - 1] = Nh[q, blocks - 1], Nl[q, blocks - 1]

                @pl.loop(1, blocks)
                def _(step):
                    b = blocks - 1 - step
                    Rh[q, b], Rl[q, b] = split(
                        compose((Nh[q, b], Nl[q, b]), (Rh[q, b + 1], Rl[q, b + 1]))
                    )

    maps_first = chip * 2 >= n

    @pl.loop(0, 3)
    def _(step):
        @pl.when(step == 1)
        def _():
            sweep_forward()

        @pl.when(step == jnp.where(maps_first, 0, 2))
        def _():
            backward_maps()

    carried = [None] * points
    for b in reversed(range(blocks)):
        for q in range(points):
            if b == blocks - 1:
                carried[q] = y[q, b]
            else:
                carried[q] = y[q, b] + apply_map(carried[q], Nh[q, b], Nl[q, b])[0]
            u[q, b] = carried[q]

    own_weights = jnp.where(core == 0, w_ref[:, :points], w_ref[:, points:])
    weight_re = [own_weights[0:1, q : q + 1] for q in range(points)]
    weight_im = [own_weights[1:2, q : q + 1] for q in range(points)]

    def filtered_part(q, x):
        return weight_re[q] * x[:vectors] - weight_im[q] * x[vectors:]

    @pl.when(last)
    def _():
        for at, copy in zip(parts, backward):
            xout[at] = piece_of(u[at[0], 0], at[1])
            copy.start()
        for b in range(blocks):
            total = filtered_part(0, u[0, b])
            for q in range(1, points):
                total = total + filtered_part(q, u[q, b])
            pf[b] = total

    @pl.when(jnp.logical_not(last))
    def _():
        for at, copy in zip(parts, backward):
            copy.wait_recv()

            @pl.when(jnp.logical_not(first))
            def _():
                known = piece_of(u[at[0], 0], at[1])
                xout[at] = known + apply_map(xin[at], Rh[at[0], 0], Rl[at[0], 0])[0]
                copy.start()

        totals = [None] * blocks
        for q in range(points):
            entering = joined([xin[q, p] for p in range(PIECES)])
            flat = (blocks * 2 * width, width)
            moved = apply_map(entering, Rh[q].reshape(flat), Rl[q].reshape(flat))
            for b in range(blocks):
                part = filtered_part(q, u[q, b] + moved[b])
                totals[b] = part if q == 0 else totals[b] + part
        for b in range(blocks):
            pf[b] = totals[b]

    share = remote(pf, pfin, one_send.at[0], one_recv.at[0], sib)
    share.start()
    share.wait_recv()
    ff[...] = pf[...] + pfin[...]

    to_left = remote(fsend, fnext, one_send.at[1], one_recv.at[1], left)
    to_right = remote(down, downin, one_send.at[2], one_recv.at[2], right)
    gives_left = jnp.logical_and(core == 0, jnp.logical_not(first))
    gives_right = jnp.logical_and(core == 1, jnp.logical_not(last))

    @pl.when(gives_left)
    def _():
        fsend[...] = ff[0]
        to_left.start()

    @pl.when(gives_right)
    def _():
        down[...] = product(split(ff[blocks - 1]), (Eh[blocks - 1], El[blocks - 1]), NN)
        to_right.start()
        to_left.wait_recv()

    @pl.when(jnp.logical_not(gives_right))
    def _():
        fnext[...] = jnp.zeros_like(fnext)

    grams = jnp.zeros((vectors, 4 * vectors), f32)
    for j in range(mine):
        at = core * mine + j
        block = ff[at]
        filt_ref[:, j * width : (j + 1) * width] = block
        if j < mine - 1:
            upper = ff[at + 1]
        else:
            upper = jnp.where(core == 0, ff[mine], fnext[...])
        halves = split(block)
        up = product(split(upper), (Eh[at], El[at]), NT)
        up_halves = split(up)
        partial = product(halves, split(D[j]), NT) + up
        blank = jnp.zeros_like(block)
        grams += product(halves, split(jnp.concatenate([block, partial, blank, blank], axis=0)), NT)
        grams += product(
            up_halves, split(jnp.concatenate([blank, block, blank, blank], axis=0)), NT
        )
        app_ref[:, j * width : (j + 1) * width] = partial

    pair = remote(gown, gsib, one_send.at[4], one_recv.at[4], sib)
    gown[...] = grams
    pass_on = remote(gown, gin, one_send.at[3], one_recv.at[3], before)

    @pl.when(jnp.logical_not(last))
    def _():
        pass_on.wait_recv()
        gown[...] = gown[...] + gin[...]

    @pl.when(jnp.logical_not(first))
    def _():
        pass_on.start()

    @pl.when(first)
    def _():
        pair.start()
        pair.wait_recv()
        scale = 1.0 / (blocks * width * n)
        gfin[...] = (gown[...] + gsib[...]) * scale

        @pl.loop(1, n)
        def _(other):
            remote(gfin, gfin, all_send.at[other], all_recv, other * 2 + core).start()

    for j in range(mine):
        at = core * mine + j
        if j == 0:
            @pl.when(core == 1)
            def _():
                below = product(split(ff[mine - 1]), (Eh[mine - 1], El[mine - 1]), NN)
                app_ref[:, :width] += below

            @pl.when(gives_left)
            def _():
                to_right.wait_recv()
                app_ref[:, :width] += downin[...]
        else:
            below = product(split(ff[at - 1]), (Eh[at - 1], El[at - 1]), NN)
            app_ref[:, j * width : (j + 1) * width] += below

    @pl.when(jnp.logical_not(first))
    def _():
        remote(gfin, gfin, all_send.at[0], all_recv, core).wait_recv()

    gram_ref[0] = gfin[:, :vectors]
    gram_ref[1] = gfin[:, vectors : 2 * vectors]

    share.wait_send()

    @pl.when(gives_left)
    def _():
        to_left.wait_send()

    @pl.when(gives_right)
    def _():
        to_right.wait_send()

    @pl.when(jnp.logical_not(last))
    def _():
        for copy in forward:
            copy.wait_send()

    @pl.when(jnp.logical_not(first))
    def _():
        for copy in backward:
            copy.wait_send()
        pass_on.wait_send()

    @pl.when(first)
    def _():
        pair.wait_send()

        @pl.loop(1, n)
        def _(other):
            remote(gfin, gfin, all_send.at[other], all_recv, other * 2 + core).wait_send()


def shards(n, subspace, s_inv, couple, diag_blocks, weights):
    points, mine = s_inv.shape[0] // 2, s_inv.shape[1]
    width, vectors = couple.shape[1], subspace.shape[0]
    blocks = 2 * mine
    pivots = s_inv.reshape(2 * points, mine, 2 * width, width)
    square = (blocks, width, width)
    maps = (points, blocks, 2 * width, width)
    state = (points, PIECES, 2 * vectors // PIECES, width)
    states = (points, blocks, 2 * vectors, width)
    piece = (vectors, width)
    grams = (2, vectors, vectors)
    scratch = (
        [pltpu.VMEM((2, vectors, mine * width), f32), pltpu.VMEM(maps, f32)]
        + [pltpu.VMEM(square, f32), pltpu.VMEM((mine, width, width), f32)]
        + [pltpu.VMEM((2, 2 * points), f32)]
        + [pltpu.VMEM(square, bf16)] * 4
        + [pltpu.VMEM((points, blocks, 4 * width, width), bf16)] * 2
        + [pltpu.VMEM(maps, bf16)] * 2
        + [pltpu.VMEM((points, 2 * width, width), bf16)] * 2
        + [pltpu.VMEM(maps, bf16)] * 2
        + [pltpu.VMEM(state, f32)] * 3
        + [pltpu.VMEM(states, f32)] * 2
        + [pltpu.VMEM(state, f32)] * 2
        + [pltpu.VMEM((blocks,) + piece, f32)] * 3
        + [pltpu.VMEM(piece, f32)] * 4
        + [pltpu.VMEM((vectors, 4 * vectors), f32)] * 4
        + [pltpu.SemaphoreType.DMA((5,))]
        + [pltpu.SemaphoreType.DMA((3,))] * 2
        + [pltpu.SemaphoreType.DMA((points, PIECES))] * 4
        + [pltpu.SemaphoreType.DMA((5,))] * 2
        + [pltpu.SemaphoreType.DMA((n,)), pltpu.SemaphoreType.DMA]
    )
    whole = pl.BlockSpec(memory_space=pltpu.VMEM)
    anywhere = pl.BlockSpec(memory_space=pl.ANY)
    return pl.pallas_call(
        functools.partial(kernel, n),
        out_shape=(
            jax.ShapeDtypeStruct(subspace.shape, f32),
            jax.ShapeDtypeStruct(subspace.shape, f32),
            jax.ShapeDtypeStruct(grams, f32),
        ),
        in_specs=[anywhere] * 5,
        out_specs=(whole, whole, whole),
        scratch_shapes=scratch,
        compiler_params=pltpu.CompilerParams(
            collective_id=0, has_side_effects=True, vmem_limit_bytes=63 * 2**20
        ),
        name="filter_pass",
    )(subspace, pivots, couple, diag_blocks, weights.T)


def solution(mesh):
    placed = (
        P("parts", "chain"),
        P("parts", "chain", None, None, None),
        P("chain", "parts", None),
        P("chain", "parts", None),
        P("parts", None),
    )
    return jax.shard_map(
        functools.partial(shards, mesh.shape["chain"] // 2),
        mesh=mesh,
        in_specs=placed,
        out_specs=(P("parts", "chain"), P("parts", "chain"), P(None, "parts", None)),
        check_vma=False,
    )
```

```python
import functools

import jax
import jax.numpy as jnp
from jax import lax
from jax.experimental import pallas as pl
from jax.experimental.pallas import tpu as pltpu
from jax.sharding import PartitionSpec as P

MESH = pl.DeviceIdType.MESH
f32, bf16 = jnp.float32, jnp.bfloat16
NT = (((1,), (1,)), ((), ()))
NN = (((1,), (0,)), ((), ()))


def split(a):
    high = a.astype(bf16)
    return high, (a - high.astype(f32)).astype(bf16)


PIECES = 4


def dot(a, b, dims):
    return lax.dot_general(a, b, dims, preferred_element_type=f32)


def product(a, b, dims):
    return dot(a[0], b[0], dims) + (dot(a[0], b[1], dims) + dot(a[1], b[0], dims))


def apply_map(rows, high, low):
    half, width = rows.shape[0] // 2, rows.shape[1]
    rows_high, rows_low = split(rows)
    both = dot(jnp.concatenate([rows_high, rows_low], axis=0), high, NT)
    mixed = both[: 2 * half] + (both[2 * half :] + dot(rows_high, low, NT))
    results = []
    for at in range(0, mixed.shape[1], 2 * width):
        by_re, by_im = mixed[:, at : at + width], mixed[:, at + width : at + 2 * width]
        results.append(
            jnp.concatenate([by_re[:half] - by_im[half:], by_re[half:] + by_im[:half]], axis=0)
        )
    return results


def apply_real(rows, high, low):
    count = rows.shape[0]
    rows_high, rows_low = split(rows)
    both = dot(jnp.concatenate([rows_high, rows_low], axis=0), high, NN)
    return both[:count] + (both[count:] + dot(rows_high, low, NN))


def joined(parts):
    half = parts[0].shape[0] // 2
    return jnp.concatenate([part[:half] for part in parts] + [part[half:] for part in parts], axis=0)


def piece_of(rows, p):
    half = rows.shape[0] // 2
    size = half // PIECES
    return jnp.concatenate(
        [rows[p * size : (p + 1) * size], rows[half + p * size : half + (p + 1) * size]], axis=0
    )


def compose(a, b):
    width = b[0].shape[1]
    by_re = product(a, (b[0][:width], b[1][:width]), NN)
    by_im = product(a, (b[0][width:], b[1][width:]), NN)
    return jnp.concatenate([by_re[:width] - by_im[width:], by_im[:width] + by_re[width:]], axis=0)


def kernel(
    n, f_hbm, s_hbm, e_hbm, d_hbm, w_hbm, filt_ref, app_ref, gram_ref,
    F, S, E, D, w_ref, Eh, El, Th, Tl, Wh, Wl, Nh, Nl, Ch, Cl, Rh, Rl,
    tip, cin, cout, y, u, xin, xout, pf, pfin, ff, fnext, fsend, down, downin,
    gown, gin, gsib, gfin, local_sem, swap_send, swap_recv, fwd_send, fwd_recv,
    bwd_send, bwd_recv, one_send, one_recv, all_send, all_recv,
):
    me = lax.axis_index("chain")
    chip, core = lax.div(me, 2), lax.rem(me, 2)
    sib = chip * 2 + 1 - core
    after = jnp.minimum(chip + 1, n - 1) * 2 + core
    before = jnp.maximum(chip - 1, 0) * 2 + core
    right = jnp.minimum(me + 1, 2 * n - 1)
    left = jnp.maximum(me - 1, 0)
    first, last = chip == 0, chip == n - 1
    near = chip < 2
    far = jnp.logical_not(near)
    points, blocks = S.shape[0], S.shape[1]
    mine = e_hbm.shape[0]
    width = e_hbm.shape[1]
    vectors = f_hbm.shape[0]

    def greet(device):
        pl.semaphore_signal(barrier, inc=1, device_id={"chain": device}, device_id_type=MESH)

    def remote(src, dst, send, recv, device):
        return pltpu.make_async_remote_copy(
            src_ref=src, dst_ref=dst, send_sem=send, recv_sem=recv,
            device_id={"chain": device}, device_id_type=MESH,
        )

    here = pl.ds(core * mine, mine)
    own_points = pl.ds(core * points, points)
    sib_points = pl.ds((1 - core) * points, points)
    local = [
        pltpu.make_async_copy(f_hbm, F.at[core], local_sem.at[0]),
        pltpu.make_async_copy(e_hbm, E.at[here], local_sem.at[1]),
        pltpu.make_async_copy(s_hbm.at[own_points], S.at[:, here], local_sem.at[2]),
        pltpu.make_async_copy(d_hbm, D, local_sem.at[3]),
        pltpu.make_async_copy(w_hbm, w_ref, local_sem.at[4]),
    ]
    for copy in local:
        copy.start()

    barrier = pltpu.get_barrier_semaphore()
    greet(sib)

    @pl.when(jnp.logical_not(first))
    def _():
        greet(before)
        greet(core)

    @pl.when(jnp.logical_not(last))
    def _():
        greet(after)

    @pl.when(jnp.logical_and(core == 0, jnp.logical_not(first)))
    def _():
        greet(left)

    @pl.when(jnp.logical_and(core == 1, jnp.logical_not(last)))
    def _():
        greet(right)

    has_next = jnp.where(last, 0, 1)
    has_prev = jnp.where(first, 0, 1)
    pl.semaphore_wait(
        barrier,
        1 + has_next + has_prev + jnp.where(core == 1, has_next, has_prev)
        + jnp.where(first, n - 1, 0),
    )
    swap = [
        remote(f_hbm, F.at[core], swap_send.at[0], swap_recv.at[0], sib),
        remote(e_hbm, E.at[here], swap_send.at[1], swap_recv.at[1], sib),
        remote(s_hbm.at[sib_points], S.at[:, here], swap_send.at[2], swap_recv.at[2], sib),
    ]
    for copy in swap:
        copy.start()
    for copy in local:
        copy.wait()

    @pl.loop(0, 2)
    def _(turn):
        @pl.when(turn == 1)
        def _():
            for copy in swap:
                copy.wait()

        start = lax.rem(core + turn, 2) * mine

        @pl.loop(0, mine)
        def _(j):
            b = start + j
            Eh[b], El[b] = split(E[b])
            turned = split(E[b].T)
            Th[b], Tl[b] = turned

            @pl.loop(0, points)
            def _(q):
                high, low = split(S[q, b])
                Wh[q, b, : 2 * width], Wl[q, b, : 2 * width] = high, low

                @pl.when(far)
                def _():
                    for part in range(2):
                        rows = slice(part * width, (part + 1) * width)
                        out = split(product(turned, (high[rows], low[rows]), NN))
                        to = slice((2 + part) * width, (3 + part) * width)
                        Wh[q, b, to], Wl[q, b, to] = out

    def source(b):
        rows = F[b // mine, :, (b % mine) * width : (b % mine + 1) * width]
        return jnp.concatenate([rows, jnp.zeros_like(rows)], axis=0)

    low_rows = slice(2 * width, 4 * width)

    @pl.when(far)
    def _():
        carried = [None] * points
        for b in range(blocks):
            for q in range(points):
                z = source(b) if b == 0 else source(b) + carried[q]
                (carried[q],) = apply_map(z, Wh[q, b, low_rows], Wl[q, b, low_rows])
        for q in range(points):
            for p in range(PIECES):
                tip[q, p] = piece_of(carried[q], p)

    @pl.when(jnp.logical_and(far, jnp.logical_not(last)))
    def _():
        @pl.loop(0, points)
        def _(q):
            Ch[q], Cl[q] = Wh[q, 0, low_rows], Wl[q, 0, low_rows]

            @pl.loop(1, blocks)
            def _(b):
                Ch[q], Cl[q] = split(
                    compose((Wh[q, b, low_rows], Wl[q, b, low_rows]), (Ch[q], Cl[q]))
                )

    parts = [(q, p) for q in range(points) for p in range(PIECES)]
    forward = [
        remote(cout.at[at], cin.at[at], fwd_send.at[at], fwd_recv.at[at], after) for at in parts
    ]
    backward = [
        remote(xout.at[at], xin.at[at], bwd_send.at[at], bwd_recv.at[at], before) for at in parts
    ]

    def entering_rows():
        return [joined([cin[q, p] for p in range(PIECES)]) for q in range(points)]

    def sweep_near():
        @pl.when(first)
        def _():
            cin[...] = jnp.zeros_like(cin)

        @pl.when(jnp.logical_not(first))
        def _():
            for copy in forward:
                copy.wait_recv()

        entering = entering_rows()
        for b in range(blocks):
            for q in range(points):
                solved = apply_map(
                    source(b) + entering[q], Wh[q, b, : 2 * width], Wl[q, b, : 2 * width]
                )[0]
                y[q, b] = solved
                entering[q] = apply_real(solved, Eh[b], El[b])

        @pl.when(jnp.logical_not(last))
        def _():
            for at, copy in zip(parts, forward):
                cout[at] = piece_of(entering[at[0]], at[1])
                copy.start()

    def sweep_far():
        for at, copy in zip(parts, forward):
            copy.wait_recv()

            @pl.when(jnp.logical_not(last))
            def _():
                cout[at] = tip[at] + apply_map(cin[at], Ch[at[0]], Cl[at[0]])[0]
                copy.start()

        entering = entering_rows()
        for b in range(blocks):
            for q in range(points):
                z = source(b) + entering[q]
                y[q, b], entering[q] = apply_map(z, Wh[q, b], Wl[q, b])

    def backward_maps():
        @pl.loop(0, points)
        def _(q):
            @pl.loop(0, blocks)
            def _(b):
                pivot = (Wh[q, b, : 2 * width], Wl[q, b, : 2 * width])
                Nh[q, b], Nl[q, b] = split(product(pivot, (Eh[b], El[b]), NN))

            @pl.when(jnp.logical_not(last))
            def _():
                Rh[q, blocks - 1], Rl[q, blocks - 1] = Nh[q, blocks - 1], Nl[q, blocks - 1]

                @pl.loop(1, blocks)
                def _(step):
                    b = blocks - 1 - step
                    Rh[q, b], Rl[q, b] = split(
                        compose((Nh[q, b], Nl[q, b]), (Rh[q, b + 1], Rl[q, b + 1]))
                    )

    maps_first = chip >= n - 2

    @pl.loop(0, 3)
    def _(step):
        @pl.when(jnp.logical_and(step == 1, near))
        def _():
            sweep_near()

        @pl.when(jnp.logical_and(step == 1, far))
        def _():
            sweep_far()

        @pl.when(step == jnp.where(maps_first, 0, 2))
        def _():
            backward_maps()

    carried = [None] * points
    for b in reversed(range(blocks)):
        for q in range(points):
            if b == blocks - 1:
                carried[q] = y[q, b]
            else:
                carried[q] = y[q, b] + apply_map(carried[q], Nh[q, b], Nl[q, b])[0]
            u[q, b] = carried[q]

    own_weights = jnp.where(core == 0, w_ref[:, :points], w_ref[:, points:])
    weight_re = [own_weights[0:1, q : q + 1] for q in range(points)]
    weight_im = [own_weights[1:2, q : q + 1] for q in range(points)]

    def filtered_part(q, x):
        return weight_re[q] * x[:vectors] - weight_im[q] * x[vectors:]

    @pl.when(last)
    def _():
        for at, copy in zip(parts, backward):
            xout[at] = piece_of(u[at[0], 0], at[1])
            copy.start()
        for b in range(blocks):
            total = filtered_part(0, u[0, b])
            for q in range(1, points):
                total = total + filtered_part(q, u[q, b])
            pf[b] = total

    @pl.when(jnp.logical_not(last))
    def _():
        for at, copy in zip(parts, backward):
            copy.wait_recv()

            @pl.when(jnp.logical_not(first))
            def _():
                known = piece_of(u[at[0], 0], at[1])
                xout[at] = known + apply_map(xin[at], Rh[at[0], 0], Rl[at[0], 0])[0]
                copy.start()

        totals = [None] * blocks
        for q in range(points):
            entering = joined([xin[q, p] for p in range(PIECES)])
            flat = (blocks * 2 * width, width)
            moved = apply_map(entering, Rh[q].reshape(flat), Rl[q].reshape(flat))
            for b in range(blocks):
                part = filtered_part(q, u[q, b] + moved[b])
                totals[b] = part if q == 0 else totals[b] + part
        for b in range(blocks):
            pf[b] = totals[b]

    share = remote(pf, pfin, one_send.at[0], one_recv.at[0], sib)
    share.start()
    share.wait_recv()
    ff[...] = pf[...] + pfin[...]

    to_left = remote(fsend, fnext, one_send.at[1], one_recv.at[1], left)
    to_right = remote(down, downin, one_send.at[2], one_recv.at[2], right)
    gives_left = jnp.logical_and(core == 0, jnp.logical_not(first))
    gives_right = jnp.logical_and(core == 1, jnp.logical_not(last))

    @pl.when(gives_left)
    def _():
        fsend[...] = ff[0]
        to_left.start()

    @pl.when(gives_right)
    def _():
        down[...] = product(split(ff[blocks - 1]), (Eh[blocks - 1], El[blocks - 1]), NN)
        to_right.start()
        to_left.wait_recv()

    @pl.when(jnp.logical_not(gives_right))
    def _():
        fnext[...] = jnp.zeros_like(fnext)

    grams = jnp.zeros((vectors, 4 * vectors), f32)
    for j in range(mine):
        at = core * mine + j
        block = ff[at]
        filt_ref[:, j * width : (j + 1) * width] = block
        if j < mine - 1:
            upper = ff[at + 1]
        else:
            upper = jnp.where(core == 0, ff[mine], fnext[...])
        halves = split(block)
        up = product(split(upper), (Eh[at], El[at]), NT)
        up_halves = split(up)
        partial = product(halves, split(D[j]), NT) + up
        blank = jnp.zeros_like(block)
        grams += product(halves, split(jnp.concatenate([block, partial, blank, blank], axis=0)), NT)
        grams += product(
            up_halves, split(jnp.concatenate([blank, block, blank, blank], axis=0)), NT
        )
        app_ref[:, j * width : (j + 1) * width] = partial

    pair = remote(gown, gsib, one_send.at[4], one_recv.at[4], sib)
    gown[...] = grams
    pass_on = remote(gown, gin, one_send.at[3], one_recv.at[3], before)

    @pl.when(jnp.logical_not(last))
    def _():
        pass_on.wait_recv()
        gown[...] = gown[...] + gin[...]

    @pl.when(jnp.logical_not(first))
    def _():
        pass_on.start()

    @pl.when(first)
    def _():
        pair.start()
        pair.wait_recv()
        scale = 1.0 / (blocks * width * n)
        gfin[...] = (gown[...] + gsib[...]) * scale

        @pl.loop(1, n)
        def _(other):
            remote(gfin, gfin, all_send.at[other], all_recv, other * 2 + core).start()

    for j in range(mine):
        at = core * mine + j
        if j == 0:
            @pl.when(core == 1)
            def _():
                below = product(split(ff[mine - 1]), (Eh[mine - 1], El[mine - 1]), NN)
                app_ref[:, :width] += below

            @pl.when(gives_left)
            def _():
                to_right.wait_recv()
                app_ref[:, :width] += downin[...]
        else:
            below = product(split(ff[at - 1]), (Eh[at - 1], El[at - 1]), NN)
            app_ref[:, j * width : (j + 1) * width] += below

    @pl.when(jnp.logical_not(first))
    def _():
        remote(gfin, gfin, all_send.at[0], all_recv, core).wait_recv()

    gram_ref[0] = gfin[:, :vectors]
    gram_ref[1] = gfin[:, vectors : 2 * vectors]

    share.wait_send()

    @pl.when(gives_left)
    def _():
        to_left.wait_send()

    @pl.when(gives_right)
    def _():
        to_right.wait_send()

    @pl.when(jnp.logical_not(last))
    def _():
        for copy in forward:
            copy.wait_send()

    @pl.when(jnp.logical_not(first))
    def _():
        for copy in backward:
            copy.wait_send()
        pass_on.wait_send()

    @pl.when(first)
    def _():
        pair.wait_send()

        @pl.loop(1, n)
        def _(other):
            remote(gfin, gfin, all_send.at[other], all_recv, other * 2 + core).wait_send()


def handing(*refs):
    sources, targets, sems = refs[:3], refs[3:6], refs[6]
    copies = [
        pltpu.make_async_copy(source, target, sems.at[i])
        for i, (source, target) in enumerate(zip(sources, targets))
    ]
    for copy in copies:
        copy.start()
    for copy in copies:
        copy.wait()


def hand_out(outputs):
    anywhere = pl.BlockSpec(memory_space=pl.ANY)
    return pl.pallas_call(
        handing,
        out_shape=tuple(jax.ShapeDtypeStruct(out.shape, out.dtype) for out in outputs),
        in_specs=[anywhere] * 3,
        out_specs=(anywhere,) * 3,
        scratch_shapes=[pltpu.SemaphoreType.DMA((3,))],
        compiler_params=pltpu.CompilerParams(vmem_limit_bytes=63 * 2**20),
        name="hand_out",
    )(*outputs)


def shards(n, subspace, s_inv, couple, diag_blocks, weights):
    points, mine = s_inv.shape[0] // 2, s_inv.shape[1]
    width, vectors = couple.shape[1], subspace.shape[0]
    blocks = 2 * mine
    pivots = s_inv.reshape(2 * points, mine, 2 * width, width)
    square = (blocks, width, width)
    maps = (points, blocks, 2 * width, width)
    state = (points, PIECES, 2 * vectors // PIECES, width)
    states = (points, blocks, 2 * vectors, width)
    piece = (vectors, width)
    grams = (2, vectors, vectors)
    scratch = (
        [pltpu.VMEM((2, vectors, mine * width), f32), pltpu.VMEM(maps, f32)]
        + [pltpu.VMEM(square, f32), pltpu.VMEM((mine, width, width), f32)]
        + [pltpu.VMEM((2, 2 * points), f32)]
        + [pltpu.VMEM(square, bf16)] * 4
        + [pltpu.VMEM((points, blocks, 4 * width, width), bf16)] * 2
        + [pltpu.VMEM(maps, bf16)] * 2
        + [pltpu.VMEM((points, 2 * width, width), bf16)] * 2
        + [pltpu.VMEM(maps, bf16)] * 2
        + [pltpu.VMEM(state, f32)] * 3
        + [pltpu.VMEM(states, f32)] * 2
        + [pltpu.VMEM(state, f32)] * 2
        + [pltpu.VMEM((blocks,) + piece, f32)] * 3
        + [pltpu.VMEM(piece, f32)] * 4
        + [pltpu.VMEM((vectors, 4 * vectors), f32)] * 4
        + [pltpu.SemaphoreType.DMA((5,))]
        + [pltpu.SemaphoreType.DMA((3,))] * 2
        + [pltpu.SemaphoreType.DMA((points, PIECES))] * 4
        + [pltpu.SemaphoreType.DMA((5,))] * 2
        + [pltpu.SemaphoreType.DMA((n,)), pltpu.SemaphoreType.DMA]
    )
    whole = pl.BlockSpec(memory_space=pltpu.VMEM)
    anywhere = pl.BlockSpec(memory_space=pl.ANY)
    outputs = pl.pallas_call(
        functools.partial(kernel, n),
        out_shape=(
            jax.ShapeDtypeStruct(subspace.shape, f32),
            jax.ShapeDtypeStruct(subspace.shape, f32),
            jax.ShapeDtypeStruct(grams, f32),
        ),
        in_specs=[anywhere] * 5,
        out_specs=(whole, whole, whole),
        scratch_shapes=scratch,
        compiler_params=pltpu.CompilerParams(
            collective_id=0, has_side_effects=True, vmem_limit_bytes=63 * 2**20
        ),
        name="filter_pass",
    )(subspace, pivots, couple, diag_blocks, weights.T)
    return tuple(hand_out(outputs))


def solution(mesh):
    placed = (
        P("parts", "chain"),
        P("parts", "chain", None, None, None),
        P("chain", "parts", None),
        P("chain", "parts", None),
        P("parts", None),
    )
    return jax.shard_map(
        functools.partial(shards, mesh.shape["chain"] // 2),
        mesh=mesh,
        in_specs=placed,
        out_specs=(P("parts", "chain"), P("parts", "chain"), P(None, "parts", None)),
        check_vma=False,
    )
```

```python
import functools

import jax
import jax.numpy as jnp
from jax import lax
from jax.experimental import pallas as pl
from jax.experimental.pallas import tpu as pltpu
from jax.sharding import PartitionSpec as P

MESH = pl.DeviceIdType.MESH
f32, bf16 = jnp.float32, jnp.bfloat16
NT = (((1,), (1,)), ((), ()))
NN = (((1,), (0,)), ((), ()))


def split(a):
    high = a.astype(bf16)
    return high, (a - high.astype(f32)).astype(bf16)


PIECES = 2


def dot(a, b, dims):
    return lax.dot_general(a, b, dims, preferred_element_type=f32)


def product(a, b, dims):
    return dot(a[0], b[0], dims) + (dot(a[0], b[1], dims) + dot(a[1], b[0], dims))


def apply_map(rows, high, low):
    half, width = rows.shape[0] // 2, rows.shape[1]
    rows_high, rows_low = split(rows)
    stacked = jnp.concatenate([rows_high, rows_low], axis=0)
    mixed = []
    for at in range(0, high.shape[0], width):
        both = dot(stacked, high[at : at + width], NN)
        fine = dot(rows_high, low[at : at + width], NN)
        mixed.append(both[: 2 * half] + (both[2 * half :] + fine))
    return [
        jnp.concatenate([by_re[:half] - by_im[half:], by_re[half:] + by_im[:half]], axis=0)
        for by_re, by_im in zip(mixed[::2], mixed[1::2])
    ]


def apply_real(rows, high, low):
    count = rows.shape[0]
    rows_high, rows_low = split(rows)
    both = dot(jnp.concatenate([rows_high, rows_low], axis=0), high, NN)
    return both[:count] + (both[count:] + dot(rows_high, low, NN))


def joined(parts):
    half = parts[0].shape[0] // 2
    return jnp.concatenate([part[:half] for part in parts] + [part[half:] for part in parts], axis=0)


def piece_of(rows, p):
    half = rows.shape[0] // 2
    size = half // PIECES
    return jnp.concatenate(
        [rows[p * size : (p + 1) * size], rows[half + p * size : half + (p + 1) * size]], axis=0
    )


def compose(a, b):
    width = b[0].shape[1]
    by_re = product(a, (b[0][:width], b[1][:width]), NN)
    by_im = product(a, (b[0][width:], b[1][width:]), NN)
    return jnp.concatenate([by_re[:width] - by_im[width:], by_im[:width] + by_re[width:]], axis=0)


def kernel(
    n, f_hbm, s_hbm, e_hbm, d_hbm, w_hbm, filt_ref, app_ref, gram_ref,
    F, S, E, D, w_ref, Eh, El, Th, Tl, Wh, Wl, Nh, Nl, Ch, Cl, Rh, Rl,
    tip, cin, cout, y, u, xin, xout, pf, pfin, ff, fnext, fsend, down, downin,
    gown, gin, gsib, gfin, local_sem, swap_send, swap_recv, fwd_send, fwd_recv,
    bwd_send, bwd_recv, one_send, one_recv, all_send, all_recv,
):
    me = lax.axis_index("chain")
    chip, core = lax.div(me, 2), lax.rem(me, 2)
    sib = chip * 2 + 1 - core
    after = jnp.minimum(chip + 1, n - 1) * 2 + core
    before = jnp.maximum(chip - 1, 0) * 2 + core
    right = jnp.minimum(me + 1, 2 * n - 1)
    left = jnp.maximum(me - 1, 0)
    first, last = chip == 0, chip == n - 1
    near = first
    far = jnp.logical_not(near)
    points, blocks = S.shape[0], S.shape[1]
    mine = e_hbm.shape[0]
    width = e_hbm.shape[1]
    vectors = f_hbm.shape[0]

    def greet(device):
        pl.semaphore_signal(barrier, inc=1, device_id={"chain": device}, device_id_type=MESH)

    def remote(src, dst, send, recv, device):
        return pltpu.make_async_remote_copy(
            src_ref=src, dst_ref=dst, send_sem=send, recv_sem=recv,
            device_id={"chain": device}, device_id_type=MESH,
        )

    here = pl.ds(core * mine, mine)
    own_points = pl.ds(core * points, points)
    sib_points = pl.ds((1 - core) * points, points)
    local = [
        pltpu.make_async_copy(f_hbm, F.at[core], local_sem.at[0]),
        pltpu.make_async_copy(e_hbm, E.at[here], local_sem.at[1]),
        pltpu.make_async_copy(s_hbm.at[own_points], S.at[:, here], local_sem.at[2]),
        pltpu.make_async_copy(d_hbm, D, local_sem.at[3]),
        pltpu.make_async_copy(w_hbm, w_ref, local_sem.at[4]),
    ]
    for copy in local:
        copy.start()

    barrier = pltpu.get_barrier_semaphore()
    greet(sib)

    @pl.when(jnp.logical_not(first))
    def _():
        greet(before)
        greet(core)

    @pl.when(jnp.logical_not(last))
    def _():
        greet(after)

    @pl.when(jnp.logical_and(core == 0, jnp.logical_not(first)))
    def _():
        greet(left)

    @pl.when(jnp.logical_and(core == 1, jnp.logical_not(last)))
    def _():
        greet(right)

    has_next = jnp.where(last, 0, 1)
    has_prev = jnp.where(first, 0, 1)
    pl.semaphore_wait(
        barrier,
        1 + has_next + has_prev + jnp.where(core == 1, has_next, has_prev)
        + jnp.where(first, n - 1, 0),
    )
    swap = [
        remote(f_hbm, F.at[core], swap_send.at[0], swap_recv.at[0], sib),
        remote(e_hbm, E.at[here], swap_send.at[1], swap_recv.at[1], sib),
        remote(s_hbm.at[sib_points], S.at[:, here], swap_send.at[2], swap_recv.at[2], sib),
    ]
    for copy in swap:
        copy.start()
    for copy in local:
        copy.wait()

    @pl.loop(0, 2)
    def _(turn):
        @pl.when(turn == 1)
        def _():
            for copy in swap:
                copy.wait()

        start = lax.rem(core + turn, 2) * mine

        @pl.loop(0, mine)
        def _(j):
            b = start + j
            Eh[b], El[b] = split(E[b])
            Th[b], Tl[b] = split(E[b].T)

            @pl.loop(0, points)
            def _(q):
                for part in range(2):
                    to = slice(part * width, (part + 1) * width)
                    Wh[q, b, to], Wl[q, b, to] = split(S[q, b, to].T)

                @pl.when(far)
                def _():
                    pivot = (Wh[q, b, : 2 * width], Wl[q, b, : 2 * width])
                    out = split(product(pivot, (Eh[b], El[b]), NN))
                    Wh[q, b, 2 * width :], Wl[q, b, 2 * width :] = out

    def source(b):
        rows = F[b // mine, :, (b % mine) * width : (b % mine + 1) * width]
        return jnp.concatenate([rows, jnp.zeros_like(rows)], axis=0)

    low_rows = slice(2 * width, 4 * width)

    @pl.when(far)
    def _():
        carried = [None] * points
        for b in range(blocks):
            for q in range(points):
                z = source(b) if b == 0 else source(b) + carried[q]
                (carried[q],) = apply_map(z, Wh[q, b, low_rows], Wl[q, b, low_rows])
        for q in range(points):
            for p in range(PIECES):
                tip[q, p] = piece_of(carried[q], p)

    @pl.when(jnp.logical_and(far, jnp.logical_not(last)))
    def _():
        @pl.loop(0, points)
        def _(q):
            Ch[q], Cl[q] = Wh[q, 0, low_rows], Wl[q, 0, low_rows]

            @pl.loop(1, blocks)
            def _(b):
                Ch[q], Cl[q] = split(
                    compose((Ch[q], Cl[q]), (Wh[q, b, low_rows], Wl[q, b, low_rows]))
                )

    parts = [(q, p) for q in range(points) for p in range(PIECES)]
    forward = [
        remote(cout.at[at], cin.at[at], fwd_send.at[at], fwd_recv.at[at], after) for at in parts
    ]
    backward = [
        remote(xout.at[at], xin.at[at], bwd_send.at[at], bwd_recv.at[at], before) for at in parts
    ]

    def entering_rows():
        return [joined([cin[q, p] for p in range(PIECES)]) for q in range(points)]

    def sweep_near():
        @pl.when(first)
        def _():
            cin[...] = jnp.zeros_like(cin)

        @pl.when(jnp.logical_not(first))
        def _():
            for copy in forward:
                copy.wait_recv()

        entering = entering_rows()
        for b in range(blocks):
            for q in range(points):
                solved = apply_map(
                    source(b) + entering[q], Wh[q, b, : 2 * width], Wl[q, b, : 2 * width]
                )[0]
                y[q, b] = solved
                entering[q] = apply_real(solved, Eh[b], El[b])

        @pl.when(jnp.logical_not(last))
        def _():
            for at, copy in zip(parts, forward):
                cout[at] = piece_of(entering[at[0]], at[1])
                copy.start()

    def sweep_far():
        for at, copy in zip(parts, forward):
            copy.wait_recv()

            @pl.when(jnp.logical_not(last))
            def _():
                cout[at] = tip[at] + apply_map(cin[at], Ch[at[0]], Cl[at[0]])[0]
                copy.start()

        entering = entering_rows()
        for b in range(blocks):
            for q in range(points):
                z = source(b) + entering[q]
                y[q, b], entering[q] = apply_map(z, Wh[q, b], Wl[q, b])

    def backward_maps():
        @pl.loop(0, points)
        def _(q):
            @pl.loop(0, blocks)
            def _(b):
                for part in range(2):
                    to = slice(part * width, (part + 1) * width)
                    turned = product((Th[b], Tl[b]), (Wh[q, b, to], Wl[q, b, to]), NN)
                    Nh[q, b, to], Nl[q, b, to] = split(turned)

            @pl.when(jnp.logical_not(last))
            def _():
                Rh[q, blocks - 1], Rl[q, blocks - 1] = Nh[q, blocks - 1], Nl[q, blocks - 1]

                @pl.loop(1, blocks)
                def _(step):
                    b = blocks - 1 - step
                    Rh[q, b], Rl[q, b] = split(
                        compose((Rh[q, b + 1], Rl[q, b + 1]), (Nh[q, b], Nl[q, b]))
                    )

    maps_first = chip * 2 >= n

    @pl.loop(0, 3)
    def _(step):
        @pl.when(jnp.logical_and(step == 1, near))
        def _():
            sweep_near()

        @pl.when(jnp.logical_and(step == 1, far))
        def _():
            sweep_far()

        @pl.when(step == jnp.where(maps_first, 0, 2))
        def _():
            backward_maps()

    carried = [None] * points
    for b in reversed(range(blocks)):
        for q in range(points):
            if b == blocks - 1:
                carried[q] = y[q, b]
            else:
                carried[q] = y[q, b] + apply_map(carried[q], Nh[q, b], Nl[q, b])[0]
            u[q, b] = carried[q]

    own_weights = jnp.where(core == 0, w_ref[:, :points], w_ref[:, points:])
    weight_re = [own_weights[0:1, q : q + 1] for q in range(points)]
    weight_im = [own_weights[1:2, q : q + 1] for q in range(points)]

    def filtered_part(q, x):
        return weight_re[q] * x[:vectors] - weight_im[q] * x[vectors:]

    @pl.when(last)
    def _():
        for at, copy in zip(parts, backward):
            xout[at] = piece_of(u[at[0], 0], at[1])
            copy.start()
        for b in range(blocks):
            total = filtered_part(0, u[0, b])
            for q in range(1, points):
                total = total + filtered_part(q, u[q, b])
            pf[b] = total

    @pl.when(jnp.logical_not(last))
    def _():
        for at, copy in zip(parts, backward):
            copy.wait_recv()

            @pl.when(jnp.logical_not(first))
            def _():
                known = piece_of(u[at[0], 0], at[1])
                xout[at] = known + apply_map(xin[at], Rh[at[0], 0], Rl[at[0], 0])[0]
                copy.start()

        totals = [None] * blocks
        for q in range(points):
            entering = joined([xin[q, p] for p in range(PIECES)])
            flat = (blocks * 2 * width, width)
            moved = apply_map(entering, Rh[q].reshape(flat), Rl[q].reshape(flat))
            for b in range(blocks):
                part = filtered_part(q, u[q, b] + moved[b])
                totals[b] = part if q == 0 else totals[b] + part
        for b in range(blocks):
            pf[b] = totals[b]

    share = remote(pf, pfin, one_send.at[0], one_recv.at[0], sib)
    share.start()
    share.wait_recv()
    ff[...] = pf[...] + pfin[...]

    to_left = remote(fsend, fnext, one_send.at[1], one_recv.at[1], left)
    to_right = remote(down, downin, one_send.at[2], one_recv.at[2], right)
    gives_left = jnp.logical_and(core == 0, jnp.logical_not(first))
    gives_right = jnp.logical_and(core == 1, jnp.logical_not(last))

    @pl.when(gives_left)
    def _():
        fsend[...] = ff[0]
        to_left.start()

    @pl.when(gives_right)
    def _():
        down[...] = product(split(ff[blocks - 1]), (Eh[blocks - 1], El[blocks - 1]), NN)
        to_right.start()
        to_left.wait_recv()

    @pl.when(jnp.logical_not(gives_right))
    def _():
        fnext[...] = jnp.zeros_like(fnext)

    grams = jnp.zeros((vectors, 4 * vectors), f32)
    for j in range(mine):
        at = core * mine + j
        block = ff[at]
        filt_ref[:, j * width : (j + 1) * width] = block
        if j < mine - 1:
            upper = ff[at + 1]
        else:
            upper = jnp.where(core == 0, ff[mine], fnext[...])
        halves = split(block)
        up = product(split(upper), (Th[at], Tl[at]), NN)
        up_halves = split(up)
        partial = product(halves, split(D[j]), NT) + up
        blank = jnp.zeros_like(block)
        grams += product(halves, split(jnp.concatenate([block, partial, blank, blank], axis=0)), NT)
        grams += product(
            up_halves, split(jnp.concatenate([blank, block, blank, blank], axis=0)), NT
        )
        app_ref[:, j * width : (j + 1) * width] = partial

    pair = remote(gown, gsib, one_send.at[4], one_recv.at[4], sib)
    gown[...] = grams
    pass_on = remote(gown, gin, one_send.at[3], one_recv.at[3], before)

    @pl.when(jnp.logical_not(last))
    def _():
        pass_on.wait_recv()
        gown[...] = gown[...] + gin[...]

    @pl.when(jnp.logical_not(first))
    def _():
        pass_on.start()

    @pl.when(first)
    def _():
        pair.start()
        pair.wait_recv()
        scale = 1.0 / (blocks * width * n)
        gfin[...] = (gown[...] + gsib[...]) * scale

        @pl.loop(1, n)
        def _(other):
            remote(gfin, gfin, all_send.at[other], all_recv, other * 2 + core).start()

    for j in range(mine):
        at = core * mine + j
        if j == 0:
            @pl.when(core == 1)
            def _():
                below = product(split(ff[mine - 1]), (Eh[mine - 1], El[mine - 1]), NN)
                app_ref[:, :width] += below

            @pl.when(gives_left)
            def _():
                to_right.wait_recv()
                app_ref[:, :width] += downin[...]
        else:
            below = product(split(ff[at - 1]), (Eh[at - 1], El[at - 1]), NN)
            app_ref[:, j * width : (j + 1) * width] += below

    @pl.when(jnp.logical_not(first))
    def _():
        remote(gfin, gfin, all_send.at[0], all_recv, core).wait_recv()

    gram_ref[0] = gfin[:, :vectors]
    gram_ref[1] = gfin[:, vectors : 2 * vectors]

    share.wait_send()

    @pl.when(gives_left)
    def _():
        to_left.wait_send()

    @pl.when(gives_right)
    def _():
        to_right.wait_send()

    @pl.when(jnp.logical_not(last))
    def _():
        for copy in forward:
            copy.wait_send()

    @pl.when(jnp.logical_not(first))
    def _():
        for copy in backward:
            copy.wait_send()
        pass_on.wait_send()

    @pl.when(first)
    def _():
        pair.wait_send()

        @pl.loop(1, n)
        def _(other):
            remote(gfin, gfin, all_send.at[other], all_recv, other * 2 + core).wait_send()


def shards(n, subspace, s_inv, couple, diag_blocks, weights):
    points, mine = s_inv.shape[0] // 2, s_inv.shape[1]
    width, vectors = couple.shape[1], subspace.shape[0]
    blocks = 2 * mine
    pivots = s_inv.reshape(2 * points, mine, 2 * width, width)
    square = (blocks, width, width)
    maps = (points, blocks, 2 * width, width)
    state = (points, PIECES, 2 * vectors // PIECES, width)
    states = (points, blocks, 2 * vectors, width)
    piece = (vectors, width)
    grams = (2, vectors, vectors)
    scratch = (
        [pltpu.VMEM((2, vectors, mine * width), f32), pltpu.VMEM(maps, f32)]
        + [pltpu.VMEM(square, f32), pltpu.VMEM((mine, width, width), f32)]
        + [pltpu.VMEM((2, 2 * points), f32)]
        + [pltpu.VMEM(square, bf16)] * 4
        + [pltpu.VMEM((points, blocks, 4 * width, width), bf16)] * 2
        + [pltpu.VMEM(maps, bf16)] * 2
        + [pltpu.VMEM((points, 2 * width, width), bf16)] * 2
        + [pltpu.VMEM(maps, bf16)] * 2
        + [pltpu.VMEM(state, f32)] * 3
        + [pltpu.VMEM(states, f32)] * 2
        + [pltpu.VMEM(state, f32)] * 2
        + [pltpu.VMEM((blocks,) + piece, f32)] * 3
        + [pltpu.VMEM(piece, f32)] * 4
        + [pltpu.VMEM((vectors, 4 * vectors), f32)] * 4
        + [pltpu.SemaphoreType.DMA((5,))]
        + [pltpu.SemaphoreType.DMA((3,))] * 2
        + [pltpu.SemaphoreType.DMA((points, PIECES))] * 4
        + [pltpu.SemaphoreType.DMA((5,))] * 2
        + [pltpu.SemaphoreType.DMA((n,)), pltpu.SemaphoreType.DMA]
    )
    whole = pl.BlockSpec(memory_space=pltpu.VMEM)
    anywhere = pl.BlockSpec(memory_space=pl.ANY)
    return pl.pallas_call(
        functools.partial(kernel, n),
        out_shape=(
            jax.ShapeDtypeStruct(subspace.shape, f32),
            jax.ShapeDtypeStruct(subspace.shape, f32),
            jax.ShapeDtypeStruct(grams, f32),
        ),
        in_specs=[anywhere] * 5,
        out_specs=(whole, whole, whole),
        scratch_shapes=scratch,
        compiler_params=pltpu.CompilerParams(
            collective_id=0, has_side_effects=True, vmem_limit_bytes=63 * 2**20
        ),
        name="filter_pass",
    )(subspace, pivots, couple, diag_blocks, weights.T)


def solution(mesh):
    placed = (
        P("parts", "chain"),
        P("parts", "chain", None, None, None),
        P("chain", "parts", None),
        P("chain", "parts", None),
        P("parts", None),
    )
    return jax.shard_map(
        functools.partial(shards, mesh.shape["chain"] // 2),
        mesh=mesh,
        in_specs=placed,
        out_specs=(P("parts", "chain"), P("parts", "chain"), P(None, "parts", None)),
        check_vma=False,
    )
```

```python
import functools

import jax
import jax.numpy as jnp
from jax import lax
from jax.experimental import pallas as pl
from jax.experimental.pallas import tpu as pltpu
from jax.sharding import PartitionSpec as P

MESH = pl.DeviceIdType.MESH
f32, bf16 = jnp.float32, jnp.bfloat16
NT = (((1,), (1,)), ((), ()))
NN = (((1,), (0,)), ((), ()))


def split(a):
    high = a.astype(bf16)
    return high, (a - high.astype(f32)).astype(bf16)


PIECES = 2


def dot(a, b, dims):
    return lax.dot_general(a, b, dims, preferred_element_type=f32)


def product(a, b, dims):
    return dot(a[0], b[0], dims) + (dot(a[0], b[1], dims) + dot(a[1], b[0], dims))


def apply_map(rows, high, low):
    half, width = rows.shape[0] // 2, rows.shape[1]
    rows_high, rows_low = split(rows)
    stacked = jnp.concatenate([rows_high, rows_low], axis=0)
    mixed = []
    for at in range(0, high.shape[0], width):
        both = dot(stacked, high[at : at + width], NN)
        fine = dot(rows_high, low[at : at + width], NN)
        mixed.append(both[: 2 * half] + (both[2 * half :] + fine))
    return [
        jnp.concatenate([by_re[:half] - by_im[half:], by_re[half:] + by_im[:half]], axis=0)
        for by_re, by_im in zip(mixed[::2], mixed[1::2])
    ]


def apply_real(rows, high, low):
    count = rows.shape[0]
    rows_high, rows_low = split(rows)
    both = dot(jnp.concatenate([rows_high, rows_low], axis=0), high, NN)
    return both[:count] + (both[count:] + dot(rows_high, low, NN))


def joined(parts):
    half = parts[0].shape[0] // 2
    return jnp.concatenate([part[:half] for part in parts] + [part[half:] for part in parts], axis=0)


def piece_of(rows, p):
    half = rows.shape[0] // 2
    size = half // PIECES
    return jnp.concatenate(
        [rows[p * size : (p + 1) * size], rows[half + p * size : half + (p + 1) * size]], axis=0
    )


def compose(a, b):
    width = b[0].shape[1]
    by_re = product(a, (b[0][:width], b[1][:width]), NN)
    by_im = product(a, (b[0][width:], b[1][width:]), NN)
    return jnp.concatenate([by_re[:width] - by_im[width:], by_im[:width] + by_re[width:]], axis=0)


def kernel(
    n, f_hbm, s_hbm, e_hbm, d_hbm, w_hbm, filt_ref, app_ref, gram_ref,
    F, S, E, D, w_ref, Eh, El, Th, Tl, Wh, Wl, Nh, Nl, Ch, Cl, Rh, Rl,
    tip, cin, cout, y, u, xin, xout, pf, pfin, ff, fnext, fsend, down, downin,
    gown, gin, gsib, gfin, local_sem, swap_send, swap_recv, fwd_send, fwd_recv,
    bwd_send, bwd_recv, one_send, one_recv, all_send, all_recv,
):
    me = lax.axis_index("chain")
    chip, core = lax.div(me, 2), lax.rem(me, 2)
    sib = chip * 2 + 1 - core
    after = jnp.minimum(chip + 1, n - 1) * 2 + core
    before = jnp.maximum(chip - 1, 0) * 2 + core
    right = jnp.minimum(me + 1, 2 * n - 1)
    left = jnp.maximum(me - 1, 0)
    first, last = chip == 0, chip == n - 1
    near = first
    far = jnp.logical_not(near)
    composed = jnp.logical_and(chip > 1, jnp.logical_not(last))
    points, blocks = S.shape[0], S.shape[1]
    mine = e_hbm.shape[0]
    width = e_hbm.shape[1]
    vectors = f_hbm.shape[0]

    def greet(device):
        pl.semaphore_signal(barrier, inc=1, device_id={"chain": device}, device_id_type=MESH)

    def remote(src, dst, send, recv, device):
        return pltpu.make_async_remote_copy(
            src_ref=src, dst_ref=dst, send_sem=send, recv_sem=recv,
            device_id={"chain": device}, device_id_type=MESH,
        )

    here = pl.ds(core * mine, mine)
    own_points = pl.ds(core * points, points)
    sib_points = pl.ds((1 - core) * points, points)
    local = [
        pltpu.make_async_copy(f_hbm, F.at[core], local_sem.at[0]),
        pltpu.make_async_copy(e_hbm, E.at[here], local_sem.at[1]),
        pltpu.make_async_copy(s_hbm.at[own_points], S.at[:, here], local_sem.at[2]),
        pltpu.make_async_copy(d_hbm, D, local_sem.at[3]),
        pltpu.make_async_copy(w_hbm, w_ref, local_sem.at[4]),
    ]
    for copy in local:
        copy.start()

    barrier = pltpu.get_barrier_semaphore()
    greet(sib)

    @pl.when(jnp.logical_not(first))
    def _():
        greet(before)
        greet(core)

    @pl.when(jnp.logical_not(last))
    def _():
        greet(after)

    @pl.when(jnp.logical_and(core == 0, jnp.logical_not(first)))
    def _():
        greet(left)

    @pl.when(jnp.logical_and(core == 1, jnp.logical_not(last)))
    def _():
        greet(right)

    has_next = jnp.where(last, 0, 1)
    has_prev = jnp.where(first, 0, 1)
    pl.semaphore_wait(
        barrier,
        1 + has_next + has_prev + jnp.where(core == 1, has_next, has_prev)
        + jnp.where(first, n - 1, 0),
    )
    swap = [
        remote(f_hbm, F.at[core], swap_send.at[0], swap_recv.at[0], sib),
        remote(e_hbm, E.at[here], swap_send.at[1], swap_recv.at[1], sib),
        remote(s_hbm.at[sib_points], S.at[:, here], swap_send.at[2], swap_recv.at[2], sib),
    ]
    for copy in swap:
        copy.start()
    for copy in local:
        copy.wait()

    @pl.loop(0, 2)
    def _(turn):
        @pl.when(turn == 1)
        def _():
            for copy in swap:
                copy.wait()

        start = lax.rem(core + turn, 2) * mine

        @pl.loop(0, mine)
        def _(j):
            b = start + j
            Eh[b], El[b] = split(E[b])
            Th[b], Tl[b] = split(E[b].T)

            @pl.loop(0, points)
            def _(q):
                for part in range(2):
                    to = slice(part * width, (part + 1) * width)
                    Wh[q, b, to], Wl[q, b, to] = split(S[q, b, to].T)

                @pl.when(far)
                def _():
                    pivot = (Wh[q, b, : 2 * width], Wl[q, b, : 2 * width])
                    out = split(product(pivot, (Eh[b], El[b]), NN))
                    Wh[q, b, 2 * width :], Wl[q, b, 2 * width :] = out

    def source(b):
        rows = F[b // mine, :, (b % mine) * width : (b % mine + 1) * width]
        return jnp.concatenate([rows, jnp.zeros_like(rows)], axis=0)

    low_rows = slice(2 * width, 4 * width)

    @pl.when(composed)
    def _():
        carried = [None] * points
        for b in range(blocks):
            for q in range(points):
                z = source(b) if b == 0 else source(b) + carried[q]
                (carried[q],) = apply_map(z, Wh[q, b, low_rows], Wl[q, b, low_rows])
        for q in range(points):
            for p in range(PIECES):
                tip[q, p] = piece_of(carried[q], p)

    @pl.when(composed)
    def _():
        @pl.loop(0, points)
        def _(q):
            Ch[q], Cl[q] = Wh[q, 0, low_rows], Wl[q, 0, low_rows]

            @pl.loop(1, blocks)
            def _(b):
                Ch[q], Cl[q] = split(
                    compose((Ch[q], Cl[q]), (Wh[q, b, low_rows], Wl[q, b, low_rows]))
                )

    parts = [(q, p) for q in range(points) for p in range(PIECES)]
    forward = [
        remote(cout.at[at], cin.at[at], fwd_send.at[at], fwd_recv.at[at], after) for at in parts
    ]
    backward = [
        remote(xout.at[at], xin.at[at], bwd_send.at[at], bwd_recv.at[at], before) for at in parts
    ]

    def entering_rows():
        return [joined([cin[q, p] for p in range(PIECES)]) for q in range(points)]

    def sweep_near():
        @pl.when(first)
        def _():
            cin[...] = jnp.zeros_like(cin)

        @pl.when(jnp.logical_not(first))
        def _():
            for copy in forward:
                copy.wait_recv()

        entering = entering_rows()
        for b in range(blocks):
            for q in range(points):
                solved = apply_map(
                    source(b) + entering[q], Wh[q, b, : 2 * width], Wl[q, b, : 2 * width]
                )[0]
                y[q, b] = solved
                entering[q] = apply_real(solved, Eh[b], El[b])

        @pl.when(jnp.logical_not(last))
        def _():
            for at, copy in zip(parts, forward):
                cout[at] = piece_of(entering[at[0]], at[1])
                copy.start()

    def sweep_far():
        for at, copy in zip(parts, forward):
            copy.wait_recv()

            @pl.when(composed)
            def _():
                cout[at] = tip[at] + apply_map(cin[at], Ch[at[0]], Cl[at[0]])[0]
                copy.start()

        entering = entering_rows()
        for b in range(blocks):
            for q in range(points):
                z = source(b) + entering[q]
                y[q, b], entering[q] = apply_map(z, Wh[q, b], Wl[q, b])

        @pl.when(jnp.logical_and(chip == 1, jnp.logical_not(last)))
        def _():
            for at, copy in zip(parts, forward):
                cout[at] = piece_of(entering[at[0]], at[1])
                copy.start()

    def backward_maps():
        @pl.loop(0, points)
        def _(q):
            @pl.loop(0, blocks)
            def _(b):
                for part in range(2):
                    to = slice(part * width, (part + 1) * width)
                    turned = product((Th[b], Tl[b]), (Wh[q, b, to], Wl[q, b, to]), NN)
                    Nh[q, b, to], Nl[q, b, to] = split(turned)

            @pl.when(jnp.logical_not(last))
            def _():
                Rh[q, blocks - 1], Rl[q, blocks - 1] = Nh[q, blocks - 1], Nl[q, blocks - 1]

                @pl.loop(1, blocks)
                def _(step):
                    b = blocks - 1 - step
                    Rh[q, b], Rl[q, b] = split(
                        compose((Rh[q, b + 1], Rl[q, b + 1]), (Nh[q, b], Nl[q, b]))
                    )

    maps_first = chip * 8 >= 5 * n

    @pl.loop(0, 3)
    def _(step):
        @pl.when(jnp.logical_and(step == 1, near))
        def _():
            sweep_near()

        @pl.when(jnp.logical_and(step == 1, far))
        def _():
            sweep_far()

        @pl.when(step == jnp.where(maps_first, 0, 2))
        def _():
            backward_maps()

    carried = [None] * points
    for b in reversed(range(blocks)):
        for q in range(points):
            if b == blocks - 1:
                carried[q] = y[q, b]
            else:
                carried[q] = y[q, b] + apply_map(carried[q], Nh[q, b], Nl[q, b])[0]
            u[q, b] = carried[q]

    own_weights = jnp.where(core == 0, w_ref[:, :points], w_ref[:, points:])
    weight_re = [own_weights[0:1, q : q + 1] for q in range(points)]
    weight_im = [own_weights[1:2, q : q + 1] for q in range(points)]

    def filtered_part(q, x):
        return weight_re[q] * x[:vectors] - weight_im[q] * x[vectors:]

    @pl.when(last)
    def _():
        for at, copy in zip(parts, backward):
            xout[at] = piece_of(u[at[0], 0], at[1])
            copy.start()
        for b in range(blocks):
            total = filtered_part(0, u[0, b])
            for q in range(1, points):
                total = total + filtered_part(q, u[q, b])
            pf[b] = total

    @pl.when(jnp.logical_not(last))
    def _():
        for at, copy in zip(parts, backward):
            copy.wait_recv()

            @pl.when(jnp.logical_not(first))
            def _():
                known = piece_of(u[at[0], 0], at[1])
                xout[at] = known + apply_map(xin[at], Rh[at[0], 0], Rl[at[0], 0])[0]
                copy.start()

        totals = [None] * blocks
        for q in range(points):
            entering = joined([xin[q, p] for p in range(PIECES)])
            flat = (blocks * 2 * width, width)
            moved = apply_map(entering, Rh[q].reshape(flat), Rl[q].reshape(flat))
            for b in range(blocks):
                part = filtered_part(q, u[q, b] + moved[b])
                totals[b] = part if q == 0 else totals[b] + part
        for b in range(blocks):
            pf[b] = totals[b]

    share = remote(pf, pfin, one_send.at[0], one_recv.at[0], sib)
    share.start()
    share.wait_recv()
    ff[...] = pf[...] + pfin[...]

    to_left = remote(fsend, fnext, one_send.at[1], one_recv.at[1], left)
    to_right = remote(down, downin, one_send.at[2], one_recv.at[2], right)
    gives_left = jnp.logical_and(core == 0, jnp.logical_not(first))
    gives_right = jnp.logical_and(core == 1, jnp.logical_not(last))

    @pl.when(gives_left)
    def _():
        fsend[...] = ff[0]
        to_left.start()

    @pl.when(gives_right)
    def _():
        down[...] = product(split(ff[blocks - 1]), (Eh[blocks - 1], El[blocks - 1]), NN)
        to_right.start()
        to_left.wait_recv()

    @pl.when(jnp.logical_not(gives_right))
    def _():
        fnext[...] = jnp.zeros_like(fnext)

    grams = jnp.zeros((vectors, 4 * vectors), f32)
    for j in range(mine):
        at = core * mine + j
        block = ff[at]
        filt_ref[:, j * width : (j + 1) * width] = block
        if j < mine - 1:
            upper = ff[at + 1]
        else:
            upper = jnp.where(core == 0, ff[mine], fnext[...])
        halves = split(block)
        up = product(split(upper), (Th[at], Tl[at]), NN)
        up_halves = split(up)
        partial = product(halves, split(D[j]), NT) + up
        blank = jnp.zeros_like(block)
        grams += product(halves, split(jnp.concatenate([block, partial, blank, blank], axis=0)), NT)
        grams += product(
            up_halves, split(jnp.concatenate([blank, block, blank, blank], axis=0)), NT
        )
        app_ref[:, j * width : (j + 1) * width] = partial

    pair = remote(gown, gsib, one_send.at[4], one_recv.at[4], sib)
    gown[...] = grams
    pass_on = remote(gown, gin, one_send.at[3], one_recv.at[3], before)

    @pl.when(jnp.logical_not(last))
    def _():
        pass_on.wait_recv()
        gown[...] = gown[...] + gin[...]

    @pl.when(jnp.logical_not(first))
    def _():
        pass_on.start()

    @pl.when(first)
    def _():
        pair.start()
        pair.wait_recv()
        scale = 1.0 / (blocks * width * n)
        gfin[...] = (gown[...] + gsib[...]) * scale

        @pl.loop(1, n)
        def _(other):
            remote(gfin, gfin, all_send.at[other], all_recv, other * 2 + core).start()

    for j in range(mine):
        at = core * mine + j
        if j == 0:
            @pl.when(core == 1)
            def _():
                below = product(split(ff[mine - 1]), (Eh[mine - 1], El[mine - 1]), NN)
                app_ref[:, :width] += below

            @pl.when(gives_left)
            def _():
                to_right.wait_recv()
                app_ref[:, :width] += downin[...]
        else:
            below = product(split(ff[at - 1]), (Eh[at - 1], El[at - 1]), NN)
            app_ref[:, j * width : (j + 1) * width] += below

    @pl.when(jnp.logical_not(first))
    def _():
        remote(gfin, gfin, all_send.at[0], all_recv, core).wait_recv()

    gram_ref[0] = gfin[:, :vectors]
    gram_ref[1] = gfin[:, vectors : 2 * vectors]

    share.wait_send()

    @pl.when(gives_left)
    def _():
        to_left.wait_send()

    @pl.when(gives_right)
    def _():
        to_right.wait_send()

    @pl.when(jnp.logical_not(last))
    def _():
        for copy in forward:
            copy.wait_send()

    @pl.when(jnp.logical_not(first))
    def _():
        for copy in backward:
            copy.wait_send()
        pass_on.wait_send()

    @pl.when(first)
    def _():
        pair.wait_send()

        @pl.loop(1, n)
        def _(other):
            remote(gfin, gfin, all_send.at[other], all_recv, other * 2 + core).wait_send()


def shards(n, subspace, s_inv, couple, diag_blocks, weights):
    points, mine = s_inv.shape[0] // 2, s_inv.shape[1]
    width, vectors = couple.shape[1], subspace.shape[0]
    blocks = 2 * mine
    pivots = s_inv.reshape(2 * points, mine, 2 * width, width)
    square = (blocks, width, width)
    maps = (points, blocks, 2 * width, width)
    state = (points, PIECES, 2 * vectors // PIECES, width)
    states = (points, blocks, 2 * vectors, width)
    piece = (vectors, width)
    grams = (2, vectors, vectors)
    scratch = (
        [pltpu.VMEM((2, vectors, mine * width), f32), pltpu.VMEM(maps, f32)]
        + [pltpu.VMEM(square, f32), pltpu.VMEM((mine, width, width), f32)]
        + [pltpu.VMEM((2, 2 * points), f32)]
        + [pltpu.VMEM(square, bf16)] * 4
        + [pltpu.VMEM((points, blocks, 4 * width, width), bf16)] * 2
        + [pltpu.VMEM(maps, bf16)] * 2
        + [pltpu.VMEM((points, 2 * width, width), bf16)] * 2
        + [pltpu.VMEM(maps, bf16)] * 2
        + [pltpu.VMEM(state, f32)] * 3
        + [pltpu.VMEM(states, f32)] * 2
        + [pltpu.VMEM(state, f32)] * 2
        + [pltpu.VMEM((blocks,) + piece, f32)] * 3
        + [pltpu.VMEM(piece, f32)] * 4
        + [pltpu.VMEM((vectors, 4 * vectors), f32)] * 4
        + [pltpu.SemaphoreType.DMA((5,))]
        + [pltpu.SemaphoreType.DMA((3,))] * 2
        + [pltpu.SemaphoreType.DMA((points, PIECES))] * 4
        + [pltpu.SemaphoreType.DMA((5,))] * 2
        + [pltpu.SemaphoreType.DMA((n,)), pltpu.SemaphoreType.DMA]
    )
    whole = pl.BlockSpec(memory_space=pltpu.VMEM)
    anywhere = pl.BlockSpec(memory_space=pl.ANY)
    return pl.pallas_call(
        functools.partial(kernel, n),
        out_shape=(
            jax.ShapeDtypeStruct(subspace.shape, f32),
            jax.ShapeDtypeStruct(subspace.shape, f32),
            jax.ShapeDtypeStruct(grams, f32),
        ),
        in_specs=[anywhere] * 5,
        out_specs=(whole, whole, whole),
        scratch_shapes=scratch,
        compiler_params=pltpu.CompilerParams(
            collective_id=0, has_side_effects=True, vmem_limit_bytes=63 * 2**20
        ),
        name="filter_pass",
    )(subspace, pivots, couple, diag_blocks, weights.T)


def solution(mesh):
    placed = (
        P("parts", "chain"),
        P("parts", "chain", None, None, None),
        P("chain", "parts", None),
        P("chain", "parts", None),
        P("parts", None),
    )
    return jax.shard_map(
        functools.partial(shards, mesh.shape["chain"] // 2),
        mesh=mesh,
        in_specs=placed,
        out_specs=(P("parts", "chain"), P("parts", "chain"), P(None, "parts", None)),
        check_vma=False,
    )
```

```python
import functools

import jax
import jax.numpy as jnp
from jax import lax
from jax.experimental import pallas as pl
from jax.experimental.pallas import tpu as pltpu
from jax.sharding import PartitionSpec as P

MESH = pl.DeviceIdType.MESH
f32, bf16 = jnp.float32, jnp.bfloat16
NT = (((1,), (1,)), ((), ()))
NN = (((1,), (0,)), ((), ()))


def split(a):
    high = a.astype(bf16)
    return high, (a - high.astype(f32)).astype(bf16)


PIECES = 4


def dot(a, b, dims):
    return lax.dot_general(a, b, dims, preferred_element_type=f32)


def product(a, b, dims):
    return dot(a[0], b[0], dims) + (dot(a[0], b[1], dims) + dot(a[1], b[0], dims))


def apply_map(rows, high, low):
    half, width = rows.shape[0] // 2, rows.shape[1]
    rows_high, rows_low = split(rows)
    stacked = jnp.concatenate([rows_high, rows_low], axis=0)
    mixed = []
    for at in range(0, high.shape[0], width):
        both = dot(stacked, high[at : at + width], NN)
        fine = dot(rows_high, low[at : at + width], NN)
        mixed.append(both[: 2 * half] + (both[2 * half :] + fine))
    return [
        jnp.concatenate([by_re[:half] - by_im[half:], by_re[half:] + by_im[:half]], axis=0)
        for by_re, by_im in zip(mixed[::2], mixed[1::2])
    ]


def apply_real(rows, high, low):
    count = rows.shape[0]
    rows_high, rows_low = split(rows)
    both = dot(jnp.concatenate([rows_high, rows_low], axis=0), high, NN)
    return both[:count] + (both[count:] + dot(rows_high, low, NN))


def joined(parts):
    half = parts[0].shape[0] // 2
    return jnp.concatenate([part[:half] for part in parts] + [part[half:] for part in parts], axis=0)


def piece_of(rows, p):
    half = rows.shape[0] // 2
    size = half // PIECES
    return jnp.concatenate(
        [rows[p * size : (p + 1) * size], rows[half + p * size : half + (p + 1) * size]], axis=0
    )


def compose(a, b):
    width = b[0].shape[1]
    by_re = product(a, (b[0][:width], b[1][:width]), NN)
    by_im = product(a, (b[0][width:], b[1][width:]), NN)
    return jnp.concatenate([by_re[:width] - by_im[width:], by_im[:width] + by_re[width:]], axis=0)


def kernel(
    n, f_hbm, s_hbm, e_hbm, d_hbm, w_hbm, filt_ref, app_ref, gram_ref,
    F, S, E, D, w_ref, Eh, El, Th, Tl, Wh, Wl, Nh, Nl, Ch, Cl, Rh, Rl,
    tip, cin, cout, y, u, xin, xout, pf, pfin, ff, fnext, fsend, down, downin,
    gown, gin, gsib, gfin, local_sem, swap_send, swap_recv, fwd_send, fwd_recv,
    bwd_send, bwd_recv, one_send, one_recv, all_send, all_recv,
):
    me = lax.axis_index("chain")
    chip, core = lax.div(me, 2), lax.rem(me, 2)
    sib = chip * 2 + 1 - core
    after = jnp.minimum(chip + 1, n - 1) * 2 + core
    before = jnp.maximum(chip - 1, 0) * 2 + core
    right = jnp.minimum(me + 1, 2 * n - 1)
    left = jnp.maximum(me - 1, 0)
    first, last = chip == 0, chip == n - 1
    near = first
    far = jnp.logical_not(near)
    points, blocks = S.shape[0], S.shape[1]
    mine = e_hbm.shape[0]
    width = e_hbm.shape[1]
    vectors = f_hbm.shape[0]

    def greet(device):
        pl.semaphore_signal(barrier, inc=1, device_id={"chain": device}, device_id_type=MESH)

    def remote(src, dst, send, recv, device):
        return pltpu.make_async_remote_copy(
            src_ref=src, dst_ref=dst, send_sem=send, recv_sem=recv,
            device_id={"chain": device}, device_id_type=MESH,
        )

    here = pl.ds(core * mine, mine)
    own_points = pl.ds(core * points, points)
    sib_points = pl.ds((1 - core) * points, points)
    local = [
        pltpu.make_async_copy(f_hbm, F.at[core], local_sem.at[0]),
        pltpu.make_async_copy(e_hbm, E.at[here], local_sem.at[1]),
        pltpu.make_async_copy(s_hbm.at[own_points], S.at[:, here], local_sem.at[2]),
        pltpu.make_async_copy(d_hbm, D, local_sem.at[3]),
        pltpu.make_async_copy(w_hbm, w_ref, local_sem.at[4]),
    ]
    for copy in local:
        copy.start()

    barrier = pltpu.get_barrier_semaphore()
    greet(sib)

    @pl.when(jnp.logical_not(first))
    def _():
        greet(before)
        greet(core)

    @pl.when(jnp.logical_not(last))
    def _():
        greet(after)

    @pl.when(jnp.logical_and(core == 0, jnp.logical_not(first)))
    def _():
        greet(left)

    @pl.when(jnp.logical_and(core == 1, jnp.logical_not(last)))
    def _():
        greet(right)

    has_next = jnp.where(last, 0, 1)
    has_prev = jnp.where(first, 0, 1)
    pl.semaphore_wait(
        barrier,
        1 + has_next + has_prev + jnp.where(core == 1, has_next, has_prev)
        + jnp.where(first, n - 1, 0),
    )
    swap = [
        remote(f_hbm, F.at[core], swap_send.at[0], swap_recv.at[0], sib),
        remote(e_hbm, E.at[here], swap_send.at[1], swap_recv.at[1], sib),
        remote(s_hbm.at[sib_points], S.at[:, here], swap_send.at[2], swap_recv.at[2], sib),
    ]
    for copy in swap:
        copy.start()
    for copy in local:
        copy.wait()

    @pl.loop(0, 2)
    def _(turn):
        @pl.when(turn == 1)
        def _():
            for copy in swap:
                copy.wait()

        start = lax.rem(core + turn, 2) * mine

        @pl.loop(0, mine)
        def _(j):
            b = start + j
            Eh[b], El[b] = split(E[b])
            Th[b], Tl[b] = split(E[b].T)

            @pl.loop(0, points)
            def _(q):
                for part in range(2):
                    to = slice(part * width, (part + 1) * width)
                    Wh[q, b, to], Wl[q, b, to] = split(S[q, b, to].T)

                @pl.when(far)
                def _():
                    pivot = (Wh[q, b, : 2 * width], Wl[q, b, : 2 * width])
                    out = split(product(pivot, (Eh[b], El[b]), NN))
                    Wh[q, b, 2 * width :], Wl[q, b, 2 * width :] = out

    def source(b):
        rows = F[b // mine, :, (b % mine) * width : (b % mine + 1) * width]
        return jnp.concatenate([rows, jnp.zeros_like(rows)], axis=0)

    low_rows = slice(2 * width, 4 * width)

    @pl.when(far)
    def _():
        carried = [None] * points
        for b in range(blocks):
            for q in range(points):
                z = source(b) if b == 0 else source(b) + carried[q]
                (carried[q],) = apply_map(z, Wh[q, b, low_rows], Wl[q, b, low_rows])
        for q in range(points):
            for p in range(PIECES):
                tip[q, p] = piece_of(carried[q], p)

    @pl.when(jnp.logical_and(far, jnp.logical_not(last)))
    def _():
        @pl.loop(0, points)
        def _(q):
            Ch[q], Cl[q] = Wh[q, 0, low_rows], Wl[q, 0, low_rows]

            @pl.loop(1, blocks)
            def _(b):
                Ch[q], Cl[q] = split(
                    compose((Ch[q], Cl[q]), (Wh[q, b, low_rows], Wl[q, b, low_rows]))
                )

    parts = [(q, p) for q in range(points) for p in range(PIECES)]
    forward = [
        remote(cout.at[at], cin.at[at], fwd_send.at[at], fwd_recv.at[at], after) for at in parts
    ]
    backward = [
        remote(xout.at[at], xin.at[at], bwd_send.at[at], bwd_recv.at[at], before) for at in parts
    ]

    def entering_rows():
        return [joined([cin[q, p] for p in range(PIECES)]) for q in range(points)]

    def sweep_near():
        @pl.when(first)
        def _():
            cin[...] = jnp.zeros_like(cin)

        @pl.when(jnp.logical_not(first))
        def _():
            for copy in forward:
                copy.wait_recv()

        entering = entering_rows()
        for b in range(blocks):
            for q in range(points):
                solved = apply_map(
                    source(b) + entering[q], Wh[q, b, : 2 * width], Wl[q, b, : 2 * width]
                )[0]
                y[q, b] = solved
                entering[q] = apply_real(solved, Eh[b], El[b])

        @pl.when(jnp.logical_not(last))
        def _():
            for at, copy in zip(parts, forward):
                cout[at] = piece_of(entering[at[0]], at[1])
                copy.start()

    def sweep_far():
        for at, copy in zip(parts, forward):
            copy.wait_recv()

            @pl.when(jnp.logical_not(last))
            def _():
                cout[at] = tip[at] + apply_map(cin[at], Ch[at[0]], Cl[at[0]])[0]
                copy.start()

        entering = entering_rows()
        for b in range(blocks):
            for q in range(points):
                z = source(b) + entering[q]
                y[q, b], entering[q] = apply_map(z, Wh[q, b], Wl[q, b])

    def backward_maps():
        @pl.loop(0, points)
        def _(q):
            @pl.loop(0, blocks)
            def _(b):
                for part in range(2):
                    to = slice(part * width, (part + 1) * width)
                    turned = product((Th[b], Tl[b]), (Wh[q, b, to], Wl[q, b, to]), NN)
                    Nh[q, b, to], Nl[q, b, to] = split(turned)

            @pl.when(jnp.logical_not(last))
            def _():
                Rh[q, blocks - 1], Rl[q, blocks - 1] = Nh[q, blocks - 1], Nl[q, blocks - 1]

                @pl.loop(1, blocks)
                def _(step):
                    b = blocks - 1 - step
                    Rh[q, b], Rl[q, b] = split(
                        compose((Rh[q, b + 1], Rl[q, b + 1]), (Nh[q, b], Nl[q, b]))
                    )

    maps_first = chip * 2 >= n

    @pl.loop(0, 3)
    def _(step):
        @pl.when(jnp.logical_and(step == 1, near))
        def _():
            sweep_near()

        @pl.when(jnp.logical_and(step == 1, far))
        def _():
            sweep_far()

        @pl.when(step == jnp.where(maps_first, 0, 2))
        def _():
            backward_maps()

    carried = [None] * points
    for b in reversed(range(blocks)):
        for q in range(points):
            if b == blocks - 1:
                carried[q] = y[q, b]
            else:
                carried[q] = y[q, b] + apply_map(carried[q], Nh[q, b], Nl[q, b])[0]
            u[q, b] = carried[q]

    own_weights = jnp.where(core == 0, w_ref[:, :points], w_ref[:, points:])
    weight_re = [own_weights[0:1, q : q + 1] for q in range(points)]
    weight_im = [own_weights[1:2, q : q + 1] for q in range(points)]

    def filtered_part(q, x):
        return weight_re[q] * x[:vectors] - weight_im[q] * x[vectors:]

    @pl.when(last)
    def _():
        for at, copy in zip(parts, backward):
            xout[at] = piece_of(u[at[0], 0], at[1])
            copy.start()
        for b in range(blocks):
            total = filtered_part(0, u[0, b])
            for q in range(1, points):
                total = total + filtered_part(q, u[q, b])
            pf[b] = total

    @pl.when(jnp.logical_not(last))
    def _():
        for at, copy in zip(parts, backward):
            copy.wait_recv()

            @pl.when(jnp.logical_not(first))
            def _():
                known = piece_of(u[at[0], 0], at[1])
                xout[at] = known + apply_map(xin[at], Rh[at[0], 0], Rl[at[0], 0])[0]
                copy.start()

        totals = [None] * blocks
        for q in range(points):
            entering = joined([xin[q, p] for p in range(PIECES)])
            flat = (blocks * 2 * width, width)
            moved = apply_map(entering, Rh[q].reshape(flat), Rl[q].reshape(flat))
            for b in range(blocks):
                part = filtered_part(q, u[q, b] + moved[b])
                totals[b] = part if q == 0 else totals[b] + part
        for b in range(blocks):
            pf[b] = totals[b]

    share = remote(pf, pfin, one_send.at[0], one_recv.at[0], sib)
    share.start()
    share.wait_recv()
    ff[...] = pf[...] + pfin[...]

    to_left = remote(fsend, fnext, one_send.at[1], one_recv.at[1], left)
    to_right = remote(down, downin, one_send.at[2], one_recv.at[2], right)
    gives_left = jnp.logical_and(core == 0, jnp.logical_not(first))
    gives_right = jnp.logical_and(core == 1, jnp.logical_not(last))

    @pl.when(gives_left)
    def _():
        fsend[...] = ff[0]
        to_left.start()

    @pl.when(gives_right)
    def _():
        down[...] = product(split(ff[blocks - 1]), (Eh[blocks - 1], El[blocks - 1]), NN)
        to_right.start()
        to_left.wait_recv()

    @pl.when(jnp.logical_not(gives_right))
    def _():
        fnext[...] = jnp.zeros_like(fnext)

    grams = jnp.zeros((vectors, 4 * vectors), f32)
    for j in range(mine):
        at = core * mine + j
        block = ff[at]
        filt_ref[:, j * width : (j + 1) * width] = block
        if j < mine - 1:
            upper = ff[at + 1]
        else:
            upper = jnp.where(core == 0, ff[mine], fnext[...])
        halves = split(block)
        up = product(split(upper), (Th[at], Tl[at]), NN)
        up_halves = split(up)
        partial = product(halves, split(D[j]), NT) + up
        blank = jnp.zeros_like(block)
        grams += product(halves, split(jnp.concatenate([block, partial, blank, blank], axis=0)), NT)
        grams += product(
            up_halves, split(jnp.concatenate([blank, block, blank, blank], axis=0)), NT
        )
        app_ref[:, j * width : (j + 1) * width] = partial

    pair = remote(gown, gsib, one_send.at[4], one_recv.at[4], sib)
    gown[...] = grams
    pass_on = remote(gown, gin, one_send.at[3], one_recv.at[3], before)

    @pl.when(jnp.logical_not(last))
    def _():
        pass_on.wait_recv()
        gown[...] = gown[...] + gin[...]

    @pl.when(jnp.logical_not(first))
    def _():
        pass_on.start()

    @pl.when(first)
    def _():
        pair.start()
        pair.wait_recv()
        scale = 1.0 / (blocks * width * n)
        gfin[...] = (gown[...] + gsib[...]) * scale

        @pl.loop(1, n)
        def _(other):
            remote(gfin, gfin, all_send.at[other], all_recv, other * 2 + core).start()

    for j in range(mine):
        at = core * mine + j
        if j == 0:
            @pl.when(core == 1)
            def _():
                below = product(split(ff[mine - 1]), (Eh[mine - 1], El[mine - 1]), NN)
                app_ref[:, :width] += below

            @pl.when(gives_left)
            def _():
                to_right.wait_recv()
                app_ref[:, :width] += downin[...]
        else:
            below = product(split(ff[at - 1]), (Eh[at - 1], El[at - 1]), NN)
            app_ref[:, j * width : (j + 1) * width] += below

    @pl.when(jnp.logical_not(first))
    def _():
        remote(gfin, gfin, all_send.at[0], all_recv, core).wait_recv()

    gram_ref[0] = gfin[:, :vectors]
    gram_ref[1] = gfin[:, vectors : 2 * vectors]

    share.wait_send()

    @pl.when(gives_left)
    def _():
        to_left.wait_send()

    @pl.when(gives_right)
    def _():
        to_right.wait_send()

    @pl.when(jnp.logical_not(last))
    def _():
        for copy in forward:
            copy.wait_send()

    @pl.when(jnp.logical_not(first))
    def _():
        for copy in backward:
            copy.wait_send()
        pass_on.wait_send()

    @pl.when(first)
    def _():
        pair.wait_send()

        @pl.loop(1, n)
        def _(other):
            remote(gfin, gfin, all_send.at[other], all_recv, other * 2 + core).wait_send()


def shards(n, subspace, s_inv, couple, diag_blocks, weights):
    points, mine = s_inv.shape[0] // 2, s_inv.shape[1]
    width, vectors = couple.shape[1], subspace.shape[0]
    blocks = 2 * mine
    pivots = s_inv.reshape(2 * points, mine, 2 * width, width)
    square = (blocks, width, width)
    maps = (points, blocks, 2 * width, width)
    state = (points, PIECES, 2 * vectors // PIECES, width)
    states = (points, blocks, 2 * vectors, width)
    piece = (vectors, width)
    grams = (2, vectors, vectors)
    scratch = (
        [pltpu.VMEM((2, vectors, mine * width), f32), pltpu.VMEM(maps, f32)]
        + [pltpu.VMEM(square, f32), pltpu.VMEM((mine, width, width), f32)]
        + [pltpu.VMEM((2, 2 * points), f32)]
        + [pltpu.VMEM(square, bf16)] * 4
        + [pltpu.VMEM((points, blocks, 4 * width, width), bf16)] * 2
        + [pltpu.VMEM(maps, bf16)] * 2
        + [pltpu.VMEM((points, 2 * width, width), bf16)] * 2
        + [pltpu.VMEM(maps, bf16)] * 2
        + [pltpu.VMEM(state, f32)] * 3
        + [pltpu.VMEM(states, f32)] * 2
        + [pltpu.VMEM(state, f32)] * 2
        + [pltpu.VMEM((blocks,) + piece, f32)] * 3
        + [pltpu.VMEM(piece, f32)] * 4
        + [pltpu.VMEM((vectors, 4 * vectors), f32)] * 4
        + [pltpu.SemaphoreType.DMA((5,))]
        + [pltpu.SemaphoreType.DMA((3,))] * 2
        + [pltpu.SemaphoreType.DMA((points, PIECES))] * 4
        + [pltpu.SemaphoreType.DMA((5,))] * 2
        + [pltpu.SemaphoreType.DMA((n,)), pltpu.SemaphoreType.DMA]
    )
    whole = pl.BlockSpec(memory_space=pltpu.VMEM)
    anywhere = pl.BlockSpec(memory_space=pl.ANY)
    return pl.pallas_call(
        functools.partial(kernel, n),
        out_shape=(
            jax.ShapeDtypeStruct(subspace.shape, f32),
            jax.ShapeDtypeStruct(subspace.shape, f32),
            jax.ShapeDtypeStruct(grams, f32),
        ),
        in_specs=[anywhere] * 5,
        out_specs=(whole, whole, whole),
        scratch_shapes=scratch,
        compiler_params=pltpu.CompilerParams(
            collective_id=0, has_side_effects=True, vmem_limit_bytes=63 * 2**20
        ),
        name="filter_pass",
    )(subspace, pivots, couple, diag_blocks, weights.T)


def solution(mesh):
    placed = (
        P("parts", "chain"),
        P("parts", "chain", None, None, None),
        P("chain", "parts", None),
        P("chain", "parts", None),
        P("parts", None),
    )
    return jax.shard_map(
        functools.partial(shards, mesh.shape["chain"] // 2),
        mesh=mesh,
        in_specs=placed,
        out_specs=(P("parts", "chain"), P("parts", "chain"), P(None, "parts", None)),
        check_vma=False,
    )
```
